128 devices in a mesh: frame: 8 (over z, y_lo), height: 8 (over y_hi, x), head: 2 (over core).
Axes of the slice: x: 4, y: 4 (y_hi: 2, y_lo: 2; y = y_hi * 2 + y_lo), z: 4, core: 2. Of those that a mesh axis runs over, the one named last changes fastest.
Arguments:
- queries: bfloat16 [16, 64, 48, 2560], P(('frame', 'head'), 'height'), may hold values from -112 to 112
- keys: bfloat16 [16, 64, 48, 2560], P(('frame', 'head'), 'height'), may hold values from -4 to 4
- values: bfloat16 [16, 64, 48, 2560], P(('frame', 'head'), 'height'), may hold values from -6 to 6
- out_weight: bfloat16 [2560, 5120], P('head'), may hold values from -0.25 to 0.25
- window_radii: int32 [20, 3], replicated, may hold values from 0 to 1
- frame_valid: int32 [16], replicated, may hold values from 0 to 1, as said below
Outputs:
- projected: bfloat16 [16, 64, 48, 5120], P(('frame', 'head'), 'height')
The draws below stay inside these ranges and needn't reach their ends.
Inputs may be any that keep to these rules, and one draw needn't show every extreme that they name: `frame_valid`: padding frames form a run of 0 to 2 frames at the start and a run of 1 to 2 frames at the end.
All inputs are finite; a program needn't handle non-finite values.
Results may differ from the reference program's by a relative error of at most 0.0057.
Values may be sent and summed in bfloat16 or wider, within the bound.
No kernel may reach another device: no remote copies, remote signals or barrier semaphores. Data moves between devices by JAX's collectives and lax.ppermute only.
A program may use at most 192 MiB of HBM per device.

```python
import jax
import jax.numpy as jnp
from jax import lax

D = 5120
HEADS = 20
HEAD_DIM = 128
COLS = 48
ROW_TILE = 2
COL_TILE = 16
NF = 16
NR = 64


def shared_keys(key):
    field = jax.random.normal(key, (NF, NR, COLS, HEADS * HEAD_DIM), jnp.float32)
    return jnp.clip(field, -4.0, 4.0)


def draw_queries(key, part):
    key_field = shared_keys(key)
    key = jax.random.fold_in(key, 1)
    result = 2.0 * jnp.clip(jax.random.normal(key, key_field.shape, jnp.float32), -4.0, 4.0)
    return result.astype(jnp.bfloat16)


def draw_keys(key, part):
    key_field = shared_keys(key)
    result = key_field
    return result.astype(jnp.bfloat16)


def draw_frame_valid(key, part):
    key = jax.random.fold_in(key, 3)
    leading = jax.random.randint(jax.random.fold_in(key, 1), (), 0, 3)
    trailing = jax.random.randint(jax.random.fold_in(key, 2), (), 1, 3)
    frame_index = jnp.arange(NF)
    return ((frame_index >= leading) & (frame_index < NF - trailing)).astype(jnp.int32)


def with_ends(array, rng, least, high):
    longest = array.shape.index(max(array.shape))
    spots = []
    for shift in (0, 1):
        where = [jax.random.randint(jax.random.fold_in(rng, axis), (), 0, length) for axis, length in enumerate(array.shape)]
        where[longest] = (where[longest] + shift) % array.shape[longest]
        spots.append(tuple(where))
    return array.at[spots[0]].set(least).at[spots[1]].set(high)


def levels(stream_key, shape, pieces, low, largest):
    loudness, own = 1.0, jax.random.fold_in(stream_key, 6)
    for dim, shards_of in pieces:
        heights = jnp.exp(jax.random.uniform(jax.random.fold_in(own, dim), (shards_of,), jnp.float32, low / len(pieces), largest / len(pieces)))
        loudness = loudness * jnp.repeat(heights, shape[dim] // shards_of).reshape([-1 if axis == dim else 1 for axis in range(len(shape))])
    return loudness


def gaussian(own_key, shape, scale, reach, shards=(), kind=jnp.bfloat16):
    drawn = jax.random.normal(own_key, shape, jnp.float32) * scale
    if len(shards) > 0:
        drawn = levels(own_key, shape, shards, -0.22, 0.18) * drawn
    return jnp.clip(drawn, min=-reach, max=reach).astype(kind)


def setup_inputs(seed: int = 0) -> dict:
    seeds = jax.random.split(jax.random.key(seed), 7)
    return {
        "queries": draw_queries(jax.random.fold_in(seeds[6], 71), 0),
        "keys": draw_keys(jax.random.fold_in(seeds[6], 71), 0),
        "values": gaussian(seeds[2], (NF, NR, COLS, HEADS * HEAD_DIM), 1.0, 6.0, ((0, 16), (1, 8))),
        "out_weight": gaussian(seeds[3], (HEADS * HEAD_DIM, D), (HEADS * HEAD_DIM // 4) ** -0.5, 0.25, ((0, 2),)),
        "window_radii": with_ends(jax.random.randint(seeds[4], (HEADS, 3), 0, 2), jax.random.fold_in(seeds[4], 1), 0, 1).astype(jnp.int32),
        "frame_valid": draw_frame_valid(jax.random.fold_in(seeds[6], 71), 0),
    }


NEG_FILL = -1.0e30


def reference(queries, keys, values, out_weight, window_radii, frame_valid):
    width = HEADS * HEAD_DIM
    pad_frames = ((1, 1), (0, 0), (0, 0), (0, 0))
    keys_pad = jnp.pad(keys, pad_frames)
    values_pad = jnp.pad(values, pad_frames)
    valid_pad = jnp.pad(frame_valid, (1, 1))
    row_tiles = jnp.arange(NR, dtype=jnp.int32) // ROW_TILE
    col_tiles = jnp.arange(COLS, dtype=jnp.int32) // COL_TILE
    row_gap = jnp.abs(row_tiles[:, None] - row_tiles[None, :])
    col_gap = jnp.abs(col_tiles[:, None] - col_tiles[None, :])
    offsets = jnp.arange(3, dtype=jnp.int32)
    query_count = NR * COLS
    key_count = 3 * NR * COLS

    def one_frame(frame):
        key_block = lax.dynamic_slice_in_dim(keys_pad, frame, 3, 0)
        value_block = lax.dynamic_slice_in_dim(values_pad, frame, 3, 0)
        valid_block = lax.dynamic_slice_in_dim(valid_pad, frame, 3, 0)
        query_block = lax.dynamic_slice_in_dim(queries, frame, 1, 0)
        query_heads = query_block.reshape(query_count, HEADS, HEAD_DIM).transpose(1, 0, 2)
        key_heads = key_block.reshape(key_count, HEADS, HEAD_DIM).transpose(1, 0, 2)
        value_heads = value_block.reshape(key_count, HEADS, HEAD_DIM).transpose(1, 0, 2)
        frame_ok = (valid_block == 1) | (offsets == 1)

        def one_head(inputs):
            head_query, head_key, head_value, radius = inputs
            frame_allow = frame_ok & (jnp.abs(offsets - 1) <= radius[0])
            row_allow = row_gap <= radius[1]
            col_allow = col_gap <= radius[2]
            allowed = (frame_allow[None, None, :, None, None]
                       & row_allow[:, None, None, :, None]
                       & col_allow[None, :, None, None, :])
            allowed = allowed.reshape(query_count, key_count)
            scores = jnp.dot(head_query, head_key.T, preferred_element_type=jnp.float32) * (HEAD_DIM ** -0.5)
            masked = jnp.where(allowed, scores, NEG_FILL)
            highest = jnp.max(masked, axis=1, keepdims=True)
            expo = jnp.exp(masked - highest)
            probs = (expo / jnp.sum(expo, axis=1, keepdims=True)).astype(jnp.bfloat16)
            return jnp.dot(probs, head_value, preferred_element_type=jnp.float32).astype(jnp.bfloat16)

        per_head = lax.map(one_head, (query_heads, key_heads, value_heads, window_radii))
        return per_head.transpose(1, 0, 2).reshape(NR, COLS, width)

    attended = lax.map(one_frame, jnp.arange(NF, dtype=jnp.int32))
    projected = jnp.dot(attended.reshape(NF * NR * COLS, width), out_weight, preferred_element_type=jnp.float32)
    return projected.astype(jnp.bfloat16).reshape(NF, NR, COLS, D)
```

```python
import functools
import math

import jax
import jax.numpy as jnp
import numpy as np
from jax import lax
from jax.experimental import pallas as pl
from jax.experimental.pallas import tpu as pltpu
from jax.sharding import PartitionSpec as P

HEAD_DIM = 128
ROW_TILE = 2
COL_TILE = 16
NEG_FILL = -1e30
GRID_AXES = ("frame", "head")
VMEM_BYTES = 56 * 1024 * 1024
SCALE = HEAD_DIM ** -0.5 * math.log2(math.e)


def copy_columns(order, sources, count, row_sets):
    def kernel(order_ref, *refs):
        ins, outs, sem = refs[: len(sources)], refs[len(sources) : -1], refs[-1]

        def copies(slot):
            columns = pl.ds(pl.multiple_of(order_ref[slot] * HEAD_DIM, HEAD_DIM), HEAD_DIM)
            for out, (start, rows) in zip(outs, row_sets):
                for which, source in enumerate(ins):
                    yield pltpu.make_async_copy(
                        source.at[pl.ds(start, rows), columns], out.at[slot, which], sem
                    )

        def begin(slot, carry):
            for copy in copies(slot):
                copy.start()
            return carry

        def end(slot, carry):
            for copy in copies(slot):
                copy.wait()
            return carry

        lax.fori_loop(0, count, begin, 0)
        lax.fori_loop(0, count, end, 0)

    return pl.pallas_call(
        kernel,
        out_shape=[
            jax.ShapeDtypeStruct((count, len(sources), rows, HEAD_DIM), sources[0].dtype)
            for _, rows in row_sets
        ],
        in_specs=[pl.BlockSpec(memory_space=pltpu.SMEM)]
        + [pl.BlockSpec(memory_space=pl.ANY)] * len(sources),
        out_specs=[pl.BlockSpec(memory_space=pl.ANY)] * len(row_sets),
        scratch_shapes=[pltpu.SemaphoreType.DMA],
    )(order, *sources)


def attend(query, keys, values, mask):
    scores = lax.dot_general(
        query, keys, (((1,), (1,)), ((), ())), preferred_element_type=jnp.float32
    )
    scores = scores * SCALE + mask
    highest = jnp.max(scores, axis=1, keepdims=True)
    expo = jnp.exp2(scores - highest)
    probs = expo * (1.0 / jnp.sum(expo, axis=1, keepdims=True))
    out = jnp.dot(probs.astype(jnp.bfloat16), values, preferred_element_type=jnp.float32)
    return out.astype(jnp.bfloat16)


def attention(meta, flags, key_info, query_col, qkv, sides, edges, corners, first, count, tile, tiles):
    tokens = tile * tiles
    total = 9 * tile

    def kernel(meta_ref, flag_ref, info_ref, qcol_ref, *refs):
        refs = list(refs)
        q_ref, k_ref, v_ref = refs[:3]
        del refs[:3]
        side_refs = [refs.pop(0) for _ in sides]
        edge_refs = [refs.pop(0) for _ in edges]
        corner_refs = [refs.pop(0) for _ in corners]
        if first:
            refs.pop(0)
        out_ref, key_buf, value_buf, col_mask = refs
        step = pl.program_id(0)
        place = step + first
        rad_f, rad_r, rad_c = meta_ref[1, place], meta_ref[2, place], meta_ref[3, place]

        @pl.when(step == 0)
        def _():
            gap = jnp.abs(qcol_ref[:, :1] - info_ref[0:1, :])
            for radius in range(2):
                col_mask[radius] = jnp.where(gap <= radius, 0.0, NEG_FILL)

        def lay(row, source_k, source_v, rows):
            key_buf[pl.ds(row, rows)] = source_k
            value_buf[pl.ds(row, rows)] = source_v

        def row_bias(band, at):
            off = jnp.zeros(band.shape, jnp.bool_)
            if at == 0:
                off = off | ((band == 0) & (flag_ref[2] == 0))
            if at == tiles - 1:
                off = off | ((band == 2) & (flag_ref[3] == 0))
            return off

        def side_bias(source):
            return ((source == 1) & (flag_ref[0] == 0)) | ((source == 2) & (flag_ref[1] == 0))

        def run(at, start, length, mask):
            rows = pl.ds(at * tile, tile)
            out_ref[rows, :] = attend(
                q_ref[rows, :], key_buf[pl.ds(start, length)], value_buf[pl.ds(start, length)], mask
            )

        if sides:

            @pl.when((rad_f > 0) & (rad_r > 0))
            def _():
                band, source = info_ref[1:2, :], info_ref[2:3, :]
                ends = [(edge_refs[0], edge_refs[1])] + [
                    (corner_refs[2 * i], corner_refs[2 * i + 1]) for i in range(2)
                ]
                for which in range(3):
                    low, high = ends[which]
                    lay(which * tile, low[0, 0], low[0, 1], tile)
                    lay((3 * (tiles + 1) + which) * tile, high[0, 0], high[0, 1], tile)
                    for at in range(tiles):
                        rows = pl.ds(at * tile, tile)
                        row = (3 * (at + 1) + which) * tile
                        if which == 0:
                            lay(row, k_ref[rows, :], v_ref[rows, :], tile)
                        else:
                            side = side_refs[which - 1]
                            lay(row, side[0, 0, rows, :], side[0, 1, rows, :], tile)
                col = col_mask[rad_c]
                for at in range(tiles):
                    bias = jnp.where(row_bias(band, at) | side_bias(source), NEG_FILL, 0.0)
                    run(at, 3 * at * tile, total, col + bias)

            @pl.when((rad_f > 0) & (rad_r == 0))
            def _():
                source = info_ref[3:4, : 3 * tile]
                for at in range(tiles):
                    rows = pl.ds(at * tile, tile)
                    lay(3 * at * tile, k_ref[rows, :], v_ref[rows, :], tile)
                    for which in (1, 2):
                        side = side_refs[which - 1]
                        lay((3 * at + which) * tile, side[0, 0, rows, :], side[0, 1, rows, :], tile)
                mask = col_mask[rad_c, :, : 3 * tile] + jnp.where(side_bias(source), NEG_FILL, 0.0)
                for at in range(tiles):
                    run(at, 3 * at * tile, 3 * tile, mask)

        @pl.when((rad_f == 0) & (rad_r > 0))
        def _():
            band = info_ref[3:4, : 3 * tile]
            lay(0, edge_refs[0][0, 0], edge_refs[0][0, 1], tile)
            lay(tile, k_ref[...], v_ref[...], tokens)
            lay(tile + tokens, edge_refs[1][0, 0], edge_refs[1][0, 1], tile)
            col = col_mask[rad_c, :, : 3 * tile]
            for at in range(tiles):
                bias = jnp.where(row_bias(band, at), NEG_FILL, 0.0)
                run(at, at * tile, 3 * tile, col + bias)

        @pl.when((rad_f == 0) & (rad_r == 0))
        def _():
            mask = col_mask[rad_c, :, :tile]
            for at in range(tiles):
                rows = pl.ds(at * tile, tile)
                out_ref[rows, :] = attend(q_ref[rows, :], k_ref[rows, :], v_ref[rows, :], mask)

    def columns(step, meta_ref, flag_ref):
        return (0, meta_ref[0, step + first])

    def by_place(limit):
        return lambda step, meta_ref, flag_ref: (jnp.minimum(step + first, limit - 1), 0, 0, 0)

    def by_slot(limit):
        return lambda step, meta_ref, flag_ref: (
            jnp.minimum(meta_ref[4, step + first], limit - 1), 0, 0, 0
        )

    def whole(step, meta_ref, flag_ref):
        return (0, 0)

    column_spec = pl.BlockSpec((tokens, HEAD_DIM), columns)
    in_specs = [pl.BlockSpec(key_info.shape, whole), pl.BlockSpec(query_col.shape, whole)]
    in_specs += [column_spec] * 3
    in_specs += [pl.BlockSpec((1,) + x.shape[1:], by_place(x.shape[0])) for x in sides]
    in_specs += [pl.BlockSpec((1,) + x.shape[1:], by_slot(x.shape[0])) for x in edges]
    in_specs += [pl.BlockSpec((1,) + x.shape[1:], by_place(x.shape[0])) for x in corners]
    operands = [key_info, query_col, *qkv[:3], *sides, *edges, *corners]
    aliases = {}
    if first:
        in_specs.append(pl.BlockSpec(memory_space=pl.ANY))
        operands.append(qkv[3])
        aliases = {2 + len(operands) - 1: 0}
    return pl.pallas_call(
        kernel,
        out_shape=jax.ShapeDtypeStruct(qkv[0].shape, jnp.bfloat16),
        grid_spec=pltpu.PrefetchScalarGridSpec(
            num_scalar_prefetch=2,
            grid=(count,),
            in_specs=in_specs,
            out_specs=column_spec,
            scratch_shapes=[
                pltpu.VMEM((3 * (tiles + 2) * tile, HEAD_DIM), jnp.bfloat16),
                pltpu.VMEM((3 * (tiles + 2) * tile, HEAD_DIM), jnp.bfloat16),
                pltpu.VMEM((2, tile, total), jnp.float32),
            ],
        ),
        input_output_aliases=aliases,
        compiler_params=pltpu.CompilerParams(vmem_limit_bytes=VMEM_BYTES),
    )(meta, flags, *operands)


def project(part, attended, own_weight, other_weight, block):
    tokens = attended.shape[0]
    depth, width = own_weight.shape

    def kernel(part_ref, own_ref, other_ref, own_w_ref, other_w_ref, out_ref):
        total = jnp.dot(own_ref[...], own_w_ref[...], preferred_element_type=jnp.float32)
        total += jnp.dot(other_ref[...], other_w_ref[...], preferred_element_type=jnp.float32)
        out_ref[...] = total.astype(out_ref.dtype)

    weight_spec = pl.BlockSpec((depth, block), lambda step, part_ref: (0, step))
    return pl.pallas_call(
        kernel,
        out_shape=jax.ShapeDtypeStruct((tokens, width), jnp.bfloat16),
        grid_spec=pltpu.PrefetchScalarGridSpec(
            num_scalar_prefetch=1,
            grid=(width // block,),
            in_specs=[
                pl.BlockSpec((tokens, depth), lambda step, part_ref: (0, part_ref[0])),
                pl.BlockSpec((tokens, depth), lambda step, part_ref: (0, 1 - part_ref[0])),
                weight_spec,
                weight_spec,
            ],
            out_specs=pl.BlockSpec((tokens, block), lambda step, part_ref: (0, step)),
        ),
        compiler_params=pltpu.CompilerParams(vmem_limit_bytes=VMEM_BYTES),
    )(part, attended, attended, own_weight, other_weight)


def on_device(queries, keys, values, out_weight, window_radii, frame_valid):
    _, rows_dev, col_total, width = queries.shape
    heads = width // HEAD_DIM
    tile = ROW_TILE * col_total
    tiles = rows_dev // ROW_TILE
    tokens = tile * tiles
    frame_pairs, height_total = lax.axis_size("frame"), lax.axis_size("height")
    frames = 2 * frame_pairs
    q, k, v = (x.reshape(tokens, width) for x in (queries, keys, values))
    outer_pairs = [(2 * i + 1, 2 * i + 2) for i in range(frame_pairs - 1)]
    outer_pairs += [(target, source) for source, target in outer_pairs]
    swap = [(0, 1), (1, 0)]
    down = [(i, i + 1) for i in range(height_total - 1)]
    up = [(i + 1, i) for i in range(height_total - 1)]

    part = lax.axis_index("head")
    frame = 2 * lax.axis_index("frame") + part
    height = lax.axis_index("height")

    index = jnp.arange(heads, dtype=jnp.int32)
    rad_f, rad_r, rad_c = window_radii[:, 0], window_radii[:, 1], window_radii[:, 2]
    rank_key = (2 * rad_f + rad_r) * heads - index
    edge_key = (2 * rad_r + rad_f) * heads - index
    rank = jnp.sum((rank_key[None, :] > rank_key[:, None]).astype(jnp.int32), axis=1)
    edge_rank = jnp.sum((edge_key[None, :] > edge_key[:, None]).astype(jnp.int32), axis=1)
    pick = (rank[None, :] == index[:, None]).astype(jnp.int32)
    features = jnp.stack((index, rad_f, rad_r, rad_c, edge_rank))
    meta = jnp.sum(features[:, None, :] * pick[None], axis=2)
    edge_order = jnp.sum((edge_rank[None, :] == index[:, None]) * index[None, :], axis=1)
    order = meta[0]

    inner, outer = frame + 1 - 2 * part, frame - 1 + 2 * part
    outer_ok = (outer >= 0) & (outer < frames) & (frame_valid[jnp.clip(outer, 0, frames - 1)] == 1)
    flags = jnp.stack(
        (frame_valid[inner] == 1, outer_ok, height > 0, height < height_total - 1)
    ).astype(jnp.int32)

    place = np.arange(9 * tile)
    key_info = np.zeros((8, 9 * tile), np.int32)
    key_info[0] = place % col_total // COL_TILE
    key_info[1] = place // (3 * tile)
    key_info[2] = place // tile % 3
    key_info[3] = place // tile
    query_col = np.broadcast_to((np.arange(tile) % col_total // COL_TILE)[:, None], (tile, 128))
    key_info, query_col = jnp.asarray(key_info), jnp.asarray(query_col.astype(np.int32))

    other_weight = lax.ppermute(out_weight, "head", swap)

    def finish(side_count, edge_count, corner_count):
        (packed,) = copy_columns(order, (k, v), side_count, [(0, tokens)])
        beyond = lax.ppermute(packed, GRID_AXES, outer_pairs)
        low, high = copy_columns(edge_order, (k, v), edge_count, [(0, tile), (tokens - tile, tile)])
        above = lax.ppermute(high, "height", down)
        below = lax.ppermute(low, "height", up)
        beside = lax.ppermute(packed, "head", swap)
        beside_above = lax.ppermute(above[:corner_count], "head", swap)
        beside_below = lax.ppermute(below[:corner_count], "head", swap)
        beyond_above = lax.ppermute(beyond[:corner_count, :, tokens - tile :], "height", down)
        beyond_below = lax.ppermute(beyond[:corner_count, :, :tile], "height", up)
        attended = attention(
            meta, flags, key_info, query_col, (q, k, v), (beside, beyond), (above, below),
            (beside_above, beside_below, beyond_above, beyond_below), 0, side_count, tile, tiles,
        )
        return project(part[None], attended, out_weight, other_weight, 512)

    projected = finish(heads, heads, heads)
    return projected.reshape(1, rows_dev, col_total, out_weight.shape[1])


def solution(mesh):
    return jax.shard_map(
        on_device,
        mesh=mesh,
        in_specs=(
            P(("frame", "head"), "height", None, None),
            P(("frame", "head"), "height", None, None),
            P(("frame", "head"), "height", None, None),
            P("head", None),
            P(),
            P(),
        ),
        out_specs=P(("frame", "head"), "height", None, None),
        check_vma=False,
    )
```

```python
import functools
import math

import jax
import jax.numpy as jnp
import numpy as np
from jax import lax
from jax.experimental import pallas as pl
from jax.experimental.pallas import tpu as pltpu
from jax.sharding import PartitionSpec as P

HEAD_DIM = 128
ROW_TILE = 2
COL_TILE = 16
NEG_FILL = -1e30
GRID_AXES = ("frame", "head")
VMEM_BYTES = 56 * 1024 * 1024
SCALE = HEAD_DIM ** -0.5 * math.log2(math.e)


def pack_heads(order, sources, groups, tile, tiles):
    tokens, width = sources[0].shape

    def kernel(order_ref, *refs):
        ins, outs = refs[: len(sources)], refs[len(sources) :]
        for (first, count, which), out in zip(groups, outs):
            for at in range(count):
                columns = pl.ds(pl.multiple_of(order_ref[first + at] * HEAD_DIM, HEAD_DIM), HEAD_DIM)
                for index, source in enumerate(which):
                    out[at, index] = ins[source][:, columns]

    return pl.pallas_call(
        kernel,
        out_shape=[
            jax.ShapeDtypeStruct((count, len(which), tokens, HEAD_DIM), sources[0].dtype)
            for _, count, which in groups
        ],
        grid_spec=pltpu.PrefetchScalarGridSpec(
            num_scalar_prefetch=1,
            grid=(tiles,),
            in_specs=[pl.BlockSpec((tile, width), lambda step, order_ref: (step, 0)) for _ in sources],
            out_specs=[
                pl.BlockSpec((count, len(which), tile, HEAD_DIM), lambda step, order_ref: (0, 0, step, 0))
                for _, count, which in groups
            ],
        ),
        compiler_params=pltpu.CompilerParams(vmem_limit_bytes=VMEM_BYTES),
    )(order, *sources)


def pack_edges(order, keys, values, count, tile, tiles):
    width = keys.shape[1]

    def kernel(order_ref, *refs):
        ins, outs = refs[:4], refs[4:]
        for at in range(count):
            columns = pl.ds(pl.multiple_of(order_ref[at] * HEAD_DIM, HEAD_DIM), HEAD_DIM)
            for edge in range(2):
                for which in range(2):
                    outs[edge][at, which] = ins[2 * edge + which][:, columns]

    def rows(at):
        return pl.BlockSpec((tile, width), lambda step, order_ref: (at, 0))

    shape = (count, 2, tile, HEAD_DIM)
    return pl.pallas_call(
        kernel,
        out_shape=[jax.ShapeDtypeStruct(shape, keys.dtype)] * 2,
        grid_spec=pltpu.PrefetchScalarGridSpec(
            num_scalar_prefetch=1,
            grid=(1,),
            in_specs=[rows(0), rows(0), rows(tiles - 1), rows(tiles - 1)],
            out_specs=[pl.BlockSpec(shape, lambda step, order_ref: (0, 0, 0, 0))] * 2,
        ),
        compiler_params=pltpu.CompilerParams(vmem_limit_bytes=VMEM_BYTES),
    )(order, keys, values, keys, values)


def attend(query, keys, values, mask):
    scores = lax.dot_general(
        query, keys, (((1,), (1,)), ((), ())), preferred_element_type=jnp.float32
    )
    scores = scores * SCALE + mask
    highest = jnp.max(scores, axis=1, keepdims=True)
    expo = jnp.exp2(scores - highest)
    probs = expo * (1.0 / jnp.sum(expo, axis=1, keepdims=True))
    out = jnp.dot(probs.astype(jnp.bfloat16), values, preferred_element_type=jnp.float32)
    return out.astype(jnp.bfloat16)


def chunk(meta, flags, key_info, query_col, query, pair, sides, edges, corners, weights, total_in,
          first, count, block, last, tile, tiles):
    tokens = tile * tiles
    span = 9 * tile
    width = weights[0].shape[1]
    blocks = width // block

    def kernel(meta_ref, flag_ref, info_ref, qcol_ref, *refs):
        refs = list(refs)
        q_ref, pair_ref = refs.pop(0), refs.pop(0)
        side_refs = [refs.pop(0) for _ in sides]
        edge_refs = [refs.pop(0) for _ in edges]
        corner_refs = [refs.pop(0) for _ in corners]
        weight_refs = [refs.pop(0) for _ in weights]
        total_ref = None if total_in is None else refs.pop(0)
        out_ref, key_buf, value_buf, col_mask, attended, weight_buf, sem = refs
        step = pl.program_id(0)
        place = jnp.minimum(step, count - 1) + first
        rad_f, rad_r, rad_c = meta_ref[1, place], meta_ref[2, place], meta_ref[3, place]

        def weight_copy(at, source):
            row = pl.multiple_of(meta_ref[6, first + at] * HEAD_DIM, HEAD_DIM)
            return pltpu.make_async_copy(
                source.at[pl.ds(row, HEAD_DIM), :],
                weight_buf.at[pl.ds(at * HEAD_DIM, HEAD_DIM), :],
                sem.at[at],
            )

        @pl.when(step == 0)
        def _():
            for at in range(count):
                own = meta_ref[5, first + at] == flag_ref[4]

                @pl.when(own)
                def _():
                    weight_copy(at, weight_refs[0]).start()

                @pl.when(jnp.logical_not(own))
                def _():
                    weight_copy(at, weight_refs[1]).start()

            gap = jnp.abs(qcol_ref[:, :1] - info_ref[0:1, :])
            for radius in range(2):
                col_mask[radius] = jnp.where(gap <= radius, 0.0, NEG_FILL)

        def lay(row, source_k, source_v, rows):
            key_buf[pl.ds(row, rows)] = source_k
            value_buf[pl.ds(row, rows)] = source_v

        def row_off(band, at):
            off = jnp.zeros(band.shape, jnp.bool_)
            if at == 0:
                off = off | ((band == 0) & (flag_ref[2] == 0))
            if at == tiles - 1:
                off = off | ((band == 2) & (flag_ref[3] == 0))
            return off

        def side_off(source):
            return ((source == 1) & (flag_ref[0] == 0)) | ((source == 2) & (flag_ref[1] == 0))

        def run(at, start, length, mask):
            rows = pl.ds(at * tile, tile)
            attended[step, rows, :] = attend(
                q_ref[0, 0, rows, :], key_buf[pl.ds(start, length)], value_buf[pl.ds(start, length)], mask
            )

        attending = step < count
        if sides:

            @pl.when(attending & (rad_f > 0) & (rad_r > 0))
            def _():
                band, source = info_ref[1:2, :], info_ref[2:3, :]
                ends = [(edge_refs[0], edge_refs[1])] + [
                    (corner_refs[2 * i], corner_refs[2 * i + 1]) for i in range(2)
                ]
                for which, body in enumerate([pair_ref] + side_refs):
                    low, high = ends[which]
                    lay(which * tile, low[0, 0], low[0, 1], tile)
                    lay((3 * (tiles + 1) + which) * tile, high[0, 0], high[0, 1], tile)
                    for at in range(tiles):
                        rows = pl.ds(at * tile, tile)
                        lay((3 * (at + 1) + which) * tile, body[0, 0, rows, :], body[0, 1, rows, :], tile)
                col = col_mask[rad_c]
                for at in range(tiles):
                    bias = jnp.where(row_off(band, at) | side_off(source), NEG_FILL, 0.0)
                    run(at, 3 * at * tile, span, col + bias)

            @pl.when(attending & (rad_f > 0) & (rad_r == 0))
            def _():
                source = info_ref[3:4, : 3 * tile]
                for which, body in enumerate([pair_ref] + side_refs):
                    for at in range(tiles):
                        rows = pl.ds(at * tile, tile)
                        lay((3 * at + which) * tile, body[0, 0, rows, :], body[0, 1, rows, :], tile)
                mask = col_mask[rad_c, :, : 3 * tile] + jnp.where(side_off(source), NEG_FILL, 0.0)
                for at in range(tiles):
                    run(at, 3 * at * tile, 3 * tile, mask)

        @pl.when(attending & (rad_f == 0) & (rad_r > 0))
        def _():
            band = info_ref[3:4, : 3 * tile]
            lay(0, edge_refs[0][0, 0], edge_refs[0][0, 1], tile)
            lay(tile, pair_ref[0, 0], pair_ref[0, 1], tokens)
            lay(tile + tokens, edge_refs[1][0, 0], edge_refs[1][0, 1], tile)
            col = col_mask[rad_c, :, : 3 * tile]
            for at in range(tiles):
                run(at, at * tile, 3 * tile, col + jnp.where(row_off(band, at), NEG_FILL, 0.0))

        @pl.when(attending & (rad_f == 0) & (rad_r == 0))
        def _():
            mask = col_mask[rad_c, :, :tile]
            for at in range(tiles):
                rows = pl.ds(at * tile, tile)
                attended[step, rows, :] = attend(
                    q_ref[0, 0, rows, :], pair_ref[0, 0, rows, :], pair_ref[0, 1, rows, :], mask
                )

        @pl.when(step == count)
        def _():
            for at in range(count):
                weight_copy(at, weight_refs[0]).wait()

        @pl.when(step >= count)
        def _():
            columns = pl.ds(pl.multiple_of((step - count) * block, block), block)
            left = jnp.concatenate([attended[at] for at in range(count)], axis=1)
            total = jnp.dot(left, weight_buf[:, columns], preferred_element_type=jnp.float32)
            if total_ref is not None:
                total += total_ref[...]
            out_ref[...] = total.astype(out_ref.dtype)

    def own_place(step):
        return jnp.minimum(step, count - 1)

    def whole(step, meta_ref, flag_ref):
        return (0, 0)

    def output_block(step, meta_ref, flag_ref):
        return (0, jnp.maximum(step - count, 0))

    def by_place(x):
        return pl.BlockSpec(
            (1,) + x.shape[1:], lambda step, meta_ref, flag_ref: (own_place(step), 0, 0, 0)
        )

    def by_slot(x):
        return pl.BlockSpec(
            (1,) + x.shape[1:],
            lambda step, meta_ref, flag_ref: (meta_ref[4, own_place(step) + first], 0, 0, 0),
        )

    in_specs = [pl.BlockSpec(key_info.shape, whole), pl.BlockSpec(query_col.shape, whole)]
    in_specs.append(
        pl.BlockSpec(
            (1,) + query.shape[1:], lambda step, meta_ref, flag_ref: (own_place(step) + first, 0, 0, 0)
        )
    )
    in_specs.append(by_place(pair))
    in_specs += [by_place(x) for x in sides]
    in_specs += [by_slot(x) for x in edges]
    in_specs += [by_place(x) for x in corners]
    in_specs += [pl.BlockSpec(memory_space=pl.ANY)] * 2
    operands = [key_info, query_col, query, pair, *sides, *edges, *corners, *weights]
    if total_in is not None:
        in_specs.append(pl.BlockSpec((tokens, block), output_block))
        operands.append(total_in)
    return pl.pallas_call(
        kernel,
        out_shape=jax.ShapeDtypeStruct((tokens, width), jnp.bfloat16 if last else jnp.float32),
        grid_spec=pltpu.PrefetchScalarGridSpec(
            num_scalar_prefetch=2,
            grid=(count + blocks,),
            in_specs=in_specs,
            out_specs=pl.BlockSpec((tokens, block), output_block),
            scratch_shapes=[
                pltpu.VMEM((3 * (tiles + 2) * tile, HEAD_DIM), jnp.bfloat16),
                pltpu.VMEM((3 * (tiles + 2) * tile, HEAD_DIM), jnp.bfloat16),
                pltpu.VMEM((2, tile, span), jnp.float32),
                pltpu.VMEM((count, tokens, HEAD_DIM), jnp.bfloat16),
                pltpu.VMEM((count * HEAD_DIM, width), jnp.bfloat16),
                pltpu.SemaphoreType.DMA((count,)),
            ],
        ),
        compiler_params=pltpu.CompilerParams(vmem_limit_bytes=VMEM_BYTES),
    )(meta, flags, *operands)


def on_device(queries, keys, values, out_weight, window_radii, frame_valid):
    _, rows_dev, col_total, width = queries.shape
    heads = width // HEAD_DIM
    tile = ROW_TILE * col_total
    tiles = rows_dev // ROW_TILE
    tokens = tile * tiles
    frame_pairs, height_total = lax.axis_size("frame"), lax.axis_size("height")
    frames = 2 * frame_pairs
    q, k, v = (x.reshape(tokens, width) for x in (queries, keys, values))
    outer_pairs = [(2 * i + 1, 2 * i + 2) for i in range(frame_pairs - 1)]
    outer_pairs += [(target, source) for source, target in outer_pairs]
    swap = [(0, 1), (1, 0)]
    down = [(i, i + 1) for i in range(height_total - 1)]
    up = [(i + 1, i) for i in range(height_total - 1)]

    part = lax.axis_index("head")
    frame = 2 * lax.axis_index("frame") + part
    height = lax.axis_index("height")

    index = jnp.arange(heads, dtype=jnp.int32)
    rad_f, rad_r, rad_c = window_radii[:, 0], window_radii[:, 1], window_radii[:, 2]
    rank_key = (2 * rad_f + rad_r) * heads - index
    edge_key = (2 * rad_r + rad_f) * heads - index
    rank = jnp.sum((rank_key[None, :] > rank_key[:, None]).astype(jnp.int32), axis=1)
    edge_rank = jnp.sum((edge_key[None, :] > edge_key[:, None]).astype(jnp.int32), axis=1)
    pick = (rank[None, :] == index[:, None]).astype(jnp.int32)
    half = heads // 2
    features = jnp.stack((index, rad_f, rad_r, rad_c, edge_rank, index // half, index % half))
    meta = jnp.sum(features[:, None, :] * pick[None], axis=2)
    edge_order = jnp.sum((edge_rank[None, :] == index[:, None]) * index[None, :], axis=1)
    order = meta[0]
    n_side, n_edge, n_corner = jnp.sum(rad_f), jnp.sum(rad_r), jnp.sum(rad_f * rad_r)

    inner, outer = frame + 1 - 2 * part, frame - 1 + 2 * part
    outer_ok = (outer >= 0) & (outer < frames) & (frame_valid[jnp.clip(outer, 0, frames - 1)] == 1)
    flags = jnp.stack(
        (frame_valid[inner] == 1, outer_ok, height > 0, height < height_total - 1, part)
    ).astype(jnp.int32)

    place = np.arange(9 * tile)
    key_info = np.zeros((8, 9 * tile), np.int32)
    key_info[0] = place % col_total // COL_TILE
    key_info[1] = place // (3 * tile)
    key_info[2] = place // tile % 3
    key_info[3] = place // tile
    query_col = np.broadcast_to((np.arange(tile) % col_total // COL_TILE)[:, None], (tile, 128))
    key_info, query_col = jnp.asarray(key_info), jnp.asarray(query_col.astype(np.int32))

    def exchange_edges(count):
        def call(k, v, edge_order):
            low, high = pack_edges(edge_order, k, v, count, tile, tiles)
            got = lax.ppermute(high, "height", down), lax.ppermute(low, "height", up)
            return tuple(jnp.pad(x, ((0, heads - count),) + ((0, 0),) * 3) for x in got)

        return call

    def exchange_corners(size, count):
        def call(beyond):
            if count == 0:
                return (jnp.zeros((size, 2, tile, HEAD_DIM), beyond.dtype),) * 2
            got = (
                lax.ppermute(beyond[:count, :, tokens - tile :], "height", down),
                lax.ppermute(beyond[:count, :, :tile], "height", up),
            )
            return tuple(jnp.pad(x, ((0, size - count),) + ((0, 0),) * 3) for x in got)

        return call

    def finish(side_count):
        def call(q, k, v, out_weight):
            sizes = split_sides(side_count)
            starts = [sum(sizes[:i]) for i in range(len(sizes))]
            rest = heads - side_count
            packed, beyond, beside = [], [], []
            if sizes:
                packed = pack_heads(order, (k, v), [(s, n, (0, 1)) for s, n in zip(starts, sizes)], tile, tiles)
                beyond = [lax.ppermute(x, GRID_AXES, outer_pairs) for x in packed]
                beside = [lax.ppermute(x, "head", swap) for x in packed]
            other_weight = lax.ppermute(out_weight, "head", swap)
            groups = [(0, heads, (0,))] + ([(side_count, rest, (1, 2))] if rest else [])
            ordered = pack_heads(order, (q, k, v), groups, tile, tiles)
            query = ordered[0]
            levels = [4, 8, 10, 12, 16, heads]
            level = sum((n_edge > x).astype(jnp.int32) for x in levels[:-1])
            edges = lax.switch(level, [exchange_edges(x) for x in levels], k, v, edge_order)
            weights = (out_weight, other_weight)
            total = None
            if rest:
                total = chunk(
                    meta, flags, key_info, query_col, query, ordered[1], (), edges, (), weights, total,
                    side_count, rest, 512, not sizes, tile, tiles,
                )
            for i, (start, size) in enumerate(zip(starts, sizes)):
                near = [lax.ppermute(x[start : start + size], "head", swap) for x in edges]
                levels = sorted({0, (size + 1) // 2, size})
                level = sum((n_corner - start > x).astype(jnp.int32) for x in levels[:-1])
                far = lax.switch(level, [exchange_corners(size, x) for x in levels], beyond[i])
                total = chunk(
                    meta, flags, key_info, query_col, query, packed[i], (beside[i], beyond[i]), edges,
                    (*near, *far), weights, total, start, size, 512, i == len(sizes) - 1, tile, tiles,
                )
            return total

        return call

    side_levels = list(range(0, heads + 1, 2))
    level = sum((n_side > x).astype(jnp.int32) for x in side_levels[:-1])
    projected = lax.switch(level, [finish(x) for x in side_levels], q, k, v, out_weight)
    return projected.reshape(1, rows_dev, col_total, out_weight.shape[1])


def split_sides(count):
    if count <= 2:
        return [count] if count else []
    if count <= 4:
        return [count - 2, 2]
    return [count - 4, 2, 2]


def solution(mesh):
    return jax.shard_map(
        on_device,
        mesh=mesh,
        in_specs=(
            P(("frame", "head"), "height", None, None),
            P(("frame", "head"), "height", None, None),
            P(("frame", "head"), "height", None, None),
            P("head", None),
            P(),
            P(),
        ),
        out_specs=P(("frame", "head"), "height", None, None),
        check_vma=False,
    )
```

```python
import functools
import math

import jax
import jax.numpy as jnp
import numpy as np
from jax import lax
from jax.experimental import pallas as pl
from jax.experimental.pallas import tpu as pltpu
from jax.sharding import PartitionSpec as P

HEAD_DIM = 128
ROW_TILE = 2
COL_TILE = 16
NEG_FILL = -1e30
GRID_AXES = ("frame", "head")
VMEM_BYTES = 62 * 1024 * 1024
SCALE = HEAD_DIM ** -0.5 * math.log2(math.e)


def plan_heads(window_radii, frame_valid, side_levels, edge_first):
    heads = window_radii.shape[0]
    frames = frame_valid.shape[0]

    def kernel(radii_ref, valid_ref, meta_ref, slot_ref, flag_ref, side_ref, edge_ref, corner_ref):
        both, side, edge = (jnp.int32(0) for _ in range(3))
        for head in range(heads):
            rad_f, rad_r = radii_ref[head, 0], radii_ref[head, 1]
            both += rad_f * rad_r
            side += rad_f * (1 - rad_r)
            edge += (1 - rad_f) * rad_r
        starts = [both + side + edge, both + side, both, 0]
        for head in range(heads):
            rad_f, rad_r = radii_ref[head, 0], radii_ref[head, 1]
            kind = 2 * rad_f + rad_r
            place = sum(jnp.where(kind == i, starts[i], 0) for i in range(4))
            slot = place + jnp.where(kind == 2, edge, 0) - jnp.where(kind == 1, side, 0)
            starts = [starts[i] + (kind == i).astype(jnp.int32) for i in range(4)]
            meta_ref[0, place] = head
            meta_ref[1, place] = rad_f
            meta_ref[2, place] = rad_r
            meta_ref[3, place] = radii_ref[head, 2]
            meta_ref[4, place] = slot
            meta_ref[5, place] = head // (heads // 2)
            meta_ref[6, place] = head % (heads // 2)
            slot_ref[slot] = head
        part = lax.axis_index("head")
        frame = 2 * lax.axis_index("frame") + part
        height = lax.axis_index("height")
        inner, outer = frame + 1 - 2 * part, frame - 1 + 2 * part
        outer_ok = (outer >= 0) & (outer < frames) & (valid_ref[jnp.clip(outer, 0, frames - 1)] == 1)
        flag_ref[0] = (valid_ref[inner] == 1).astype(jnp.int32)
        flag_ref[1] = outer_ok.astype(jnp.int32)
        flag_ref[2] = (height > 0).astype(jnp.int32)
        flag_ref[3] = (height < lax.axis_size("height") - 1).astype(jnp.int32)
        flag_ref[4] = part
        fits = [jnp.where(x >= both + side, x, heads + 1) for x in side_levels]
        least = functools.reduce(jnp.minimum, fits)
        side_ref[0] = sum(jnp.where(x == least, i, 0) for i, x in enumerate(side_levels))
        edge_ref[0] = (both + edge > edge_first).astype(jnp.int32)
        corner_ref[0] = both

    smem = pl.BlockSpec(memory_space=pltpu.SMEM)
    shapes = [(8, heads), (heads,), (8,), (1,), (1,), (1,)]
    return pl.pallas_call(
        kernel,
        out_shape=[jax.ShapeDtypeStruct(shape, jnp.int32) for shape in shapes],
        in_specs=[smem, smem],
        out_specs=[smem] * len(shapes),
    )(window_radii, frame_valid)


def pack_heads(order, sources, groups, tile, tiles, slots=None, edge_count=0):
    tokens, width = sources[0].shape
    scalars = [order] if slots is None else [order, slots]
    edge_shape = (edge_count, len(sources), tile, HEAD_DIM)

    def kernel(*refs):
        order_ref, refs = refs[0], refs[len(scalars) - 1 :]
        slot_ref, refs = refs[0], refs[1:]
        ins, outs = refs[: len(sources)], refs[len(sources) :]

        def gather(from_ref, first, count, which, out):
            def copy(at, carry):
                columns = pl.ds(pl.multiple_of(from_ref[first + at] * HEAD_DIM, HEAD_DIM), HEAD_DIM)
                for index, source in enumerate(which):
                    out[at, index] = ins[source][:, columns]
                return carry

            lax.fori_loop(0, count, copy, 0, unroll=2)

        for (first, count, which), out in zip(groups, outs):
            gather(order_ref, first, count, which, out)
        if slots is not None:
            for at, out in zip((0, tiles - 1), outs[len(groups) :]):

                @pl.when(pl.program_id(0) == at)
                def _():
                    gather(slot_ref, 0, edge_count, range(len(sources)), out)

    in_spec = pl.BlockSpec((tile, width), lambda step, *refs: (step, 0))
    out_specs = [
        pl.BlockSpec((count, len(which), tile, HEAD_DIM), lambda step, *refs: (0, 0, step, 0))
        for _, count, which in groups
    ]
    shapes = [(count, len(which), tokens, HEAD_DIM) for _, count, which in groups]
    if slots is not None:
        out_specs += [pl.BlockSpec(edge_shape, lambda step, *refs: (0, 0, 0, 0))] * 2
        shapes += [edge_shape] * 2
    return pl.pallas_call(
        kernel,
        out_shape=[jax.ShapeDtypeStruct(shape, sources[0].dtype) for shape in shapes],
        grid_spec=pltpu.PrefetchScalarGridSpec(
            num_scalar_prefetch=len(scalars),
            grid=(tiles,),
            in_specs=[in_spec] * len(sources),
            out_specs=out_specs,
        ),
        compiler_params=pltpu.CompilerParams(vmem_limit_bytes=VMEM_BYTES),
    )(*scalars, *sources)


def pack_edges(order, keys, values, first, count, tile, tiles):
    width = keys.shape[1]

    def kernel(order_ref, *refs):
        ins, outs = refs[:4], refs[4:]
        def copy(at, carry):
            columns = pl.ds(pl.multiple_of(order_ref[first + at] * HEAD_DIM, HEAD_DIM), HEAD_DIM)
            for edge in range(2):
                for which in range(2):
                    outs[edge][at, which] = ins[2 * edge + which][:, columns]
            return carry

        lax.fori_loop(0, count, copy, 0)

    def rows(at):
        return pl.BlockSpec((tile, width), lambda step, order_ref: (at, 0))

    shape = (count, 2, tile, HEAD_DIM)
    return pl.pallas_call(
        kernel,
        out_shape=[jax.ShapeDtypeStruct(shape, keys.dtype)] * 2,
        grid_spec=pltpu.PrefetchScalarGridSpec(
            num_scalar_prefetch=1,
            grid=(1,),
            in_specs=[rows(0), rows(0), rows(tiles - 1), rows(tiles - 1)],
            out_specs=[pl.BlockSpec(shape, lambda step, order_ref: (0, 0, 0, 0))] * 2,
        ),
        compiler_params=pltpu.CompilerParams(vmem_limit_bytes=VMEM_BYTES),
    )(order, keys, values, keys, values)


def attend(query, keys, values, col_mask, biases, flip):
    scores = lax.dot_general(
        keys, query, (((1,), (1,)), ((), ())), preferred_element_type=jnp.float32
    )
    mask = jnp.concatenate([col_mask if x is None else col_mask + x for x in biases], axis=0)
    scores = scores * SCALE + mask
    expo = jnp.exp2(scores - jnp.max(scores, axis=0, keepdims=True))
    probs = (expo * (1.0 / jnp.sum(expo, axis=0, keepdims=True))).astype(jnp.bfloat16)
    left, right = (values, probs) if flip else (probs, values)
    out = lax.dot_general(left, right, (((0,), (0,)), ((), ())), preferred_element_type=jnp.float32)
    return (out.T if flip else out).astype(jnp.bfloat16)


def chunk(meta, flags, col_masks, first, own, given, weights, total_in, last, block, tile, tiles, unroll=2):
    tokens = tile * tiles
    count = own["query"].shape[0] if own else 0
    sides, corners = (own.get("sides", ()), own.get("corners", ())) if own else ((), ())
    edges = own["edges"] if own else ()
    split = edges[0][0].shape[0] if own else 0
    places = [(start + i, g, i) for g, (start, x) in enumerate(given) for i in range(x.shape[0])]
    places += [(first + i, None, i) for i in range(count)]
    depth = len(places)
    width = weights[0].shape[1] if weights else 0
    blocks = width // block
    across = 1 + len(sides)

    def kernel(meta_ref, flag_ref, mask_ref, *refs):
        refs = list(refs)

        def take(items):
            return [refs.pop(0) for _ in items]

        query_ref, pair_ref = take(range(2)) if own else (None, None)
        side_refs, corner_refs = take(sides), take(corners)
        edge_refs = [take(part) for part in edges]
        given_refs, weight_refs = take(given), take(weights)
        total_ref = refs.pop(0) if total_in is not None else None
        out_ref = refs.pop(0)
        if own:
            query_buf, pair_buf, edge_buf, key_buf, value_buf, attended, own_sem, edge_sem = take(range(8))
        side_buf, corner_buf = take(sides[:1]), take(corners[:1])
        given_bufs = take(given)
        if given:
            given_sem = refs.pop(0)
        if weights:
            weight_buf, weight_sem, out_buf, out_sem = take(range(4))
        if total_ref is not None:
            total_buf, total_sem = take(range(2))

        def own_copies(at):
            pairs = [(query_ref.at[at], query_buf.at[at]), (pair_ref.at[at], pair_buf.at[at])]
            pairs += [(x.at[at], side_buf[0].at[at, i]) for i, x in enumerate(side_refs)]
            pairs += [(x.at[at], corner_buf[0].at[at, i]) for i, x in enumerate(corner_refs)]
            return [pltpu.make_async_copy(x, y, own_sem.at[at, i]) for i, (x, y) in enumerate(pairs)]

        def edge_copies(at, part, slot):
            return [
                pltpu.make_async_copy(x.at[slot], edge_buf.at[at, i], edge_sem.at[at, i])
                for i, x in enumerate(edge_refs[part])
            ]

        def begin_own(at, carry):
            for copy in own_copies(at):
                copy.start()
            slot = meta_ref[4, first + at]

            @pl.when(slot < split)
            def _():
                for copy in edge_copies(at, 0, slot):
                    copy.start()

            @pl.when(slot >= split)
            def _():
                for copy in edge_copies(at, 1, slot - split):
                    copy.start()

            return carry

        def given_copy(g):
            return pltpu.make_async_copy(given_refs[g], given_bufs[g], given_sem.at[g])

        def columns(at):
            return pl.ds(pl.multiple_of(at * block, block), block)

        def weight_copy(index, at, source):
            row = pl.multiple_of(meta_ref[6, places[index][0]] * HEAD_DIM, HEAD_DIM)
            return pltpu.make_async_copy(
                source.at[pl.ds(row, HEAD_DIM), columns(at)],
                weight_buf.at[pl.ds(index * HEAD_DIM, HEAD_DIM), columns(at)],
                weight_sem.at[index, at],
            )

        def total_copy(at):
            return pltpu.make_async_copy(total_ref.at[:, columns(at)], total_buf.at[:, columns(at)], total_sem.at[at])

        def out_copy(at):
            return pltpu.make_async_copy(out_buf.at[:, columns(at)], out_ref.at[:, columns(at)], out_sem.at[at])

        def begin_share(at, carry):
            for index in range(depth):
                mine = meta_ref[5, places[index][0]] == flag_ref[4]

                @pl.when(mine)
                def _():
                    weight_copy(index, at, weight_refs[0]).start()

                @pl.when(jnp.logical_not(mine))
                def _():
                    weight_copy(index, at, weight_refs[1]).start()

            if total_ref is not None:
                total_copy(at).start()
            return carry

        def tile_rows(at, size=1):
            return pl.ds(pl.multiple_of(at * tile, tile), size * tile)

        def off(ok):
            return jnp.where(ok, 0.0, NEG_FILL)

        def lay(row, source_k, source_v):
            key_buf[tile_rows(row), :] = source_k
            value_buf[tile_rows(row), :] = source_v

        def head_step(head, carry):
            place = first + head
            rad_f, rad_r, rad_c = meta_ref[1, place], meta_ref[2, place], meta_ref[3, place]
            for copy in own_copies(head) + edge_copies(head, 0, 0):
                copy.wait()
            col_mask = mask_ref[rad_c]
            side_bias = [None] + [off((rad_f > 0) & (flag_ref[i] != 0)) for i in range(across - 1)]
            bodies = [pair_buf.at[head]] + [side_buf[0].at[head, i] for i in range(across - 1)]

            def band_bias(at):
                low = off((rad_r > 0) & ((at > 0) | (flag_ref[2] != 0)))
                high = off((rad_r > 0) & ((at < tiles - 1) | (flag_ref[3] != 0)))
                return low, None, high

            def run(at, start, biases, flip):
                rows, held = tile_rows(at), tile_rows(start, len(biases))
                attended[head, rows, :] = attend(
                    query_buf[head, 0, rows, :], key_buf[held, :], value_buf[held, :], col_mask, biases, flip
                )

            def fill(band):
                def step(at, carry):
                    rows = tile_rows(at)
                    for which, body in enumerate(bodies):
                        lay(across * (at + band) + which, body[0, rows, :], body[1, rows, :])
                    return carry

                lax.fori_loop(0, tiles, step, 0, unroll=2)

            def with_rows():
                ends = [(edge_buf.at[head, 2 * i], edge_buf.at[head, 2 * i + 1]) for i in range(len(edges[0]) // 2)]
                if corners:
                    ends.append((corner_buf[0].at[head, 0], corner_buf[0].at[head, 1]))
                for which, (low, high) in enumerate(ends):
                    lay(which, low[0], low[1])
                    lay(across * (tiles + 1) + which, high[0], high[1])
                fill(1)

                def each(at, carry):
                    biases = []
                    for x in band_bias(at):
                        for y in side_bias:
                            biases.append(x if y is None else y if x is None else jnp.minimum(x, y))
                    run(at, across * at, biases, across > 1)
                    return carry

                lax.fori_loop(0, tiles, each, 0, unroll=tiles if across == 1 else unroll)

            if sides:
                pl.when(rad_r > 0)(with_rows)

                @pl.when(rad_r == 0)
                def _():
                    fill(0)

                    def each(at, carry):
                        run(at, across * at, side_bias, False)
                        return carry

                    lax.fori_loop(0, tiles, each, 0, unroll=tiles)

            else:
                with_rows()
            return carry

        def share(at, carry):
            for index in range(depth):
                weight_copy(index, at, weight_refs[0]).wait()
            held = [attended[i] if g is None else given_bufs[g][i] for _, g, i in places]
            left = jnp.concatenate(held, axis=1)
            total = jnp.dot(left, weight_buf[:, columns(at)], preferred_element_type=jnp.float32)
            if total_ref is not None:
                total_copy(at).wait()
                total += total_buf[:, columns(at)]
            out_buf[:, columns(at)] = total.astype(out_buf.dtype)
            out_copy(at).start()
            return carry

        def end_share(at, carry):
            out_copy(at).wait()
            return carry

        if own:
            lax.fori_loop(0, count, begin_own, 0)
        for g in range(len(given)):
            given_copy(g).start()
        if weights:
            lax.fori_loop(0, blocks, begin_share, 0)
        if own:
            lax.fori_loop(0, count, head_step, 0)
        for g in range(len(given)):
            given_copy(g).wait()
        if weights:
            lax.fori_loop(0, blocks, share, 0)
            lax.fori_loop(0, blocks, end_share, 0)
        else:
            done = pltpu.make_async_copy(attended, out_ref, own_sem.at[0, 0])
            done.start()
            done.wait()

    anywhere, smem = pl.BlockSpec(memory_space=pl.ANY), pl.BlockSpec(memory_space=pltpu.SMEM)
    operands, scratch = [], []
    bf16 = jnp.bfloat16
    if own:
        operands += [own["query"], own["pair"], *sides, *corners, *edges[0], *edges[1]]
        kinds = 2 + len(sides) + len(corners)
        scratch += [
            pltpu.VMEM(own["query"].shape, bf16),
            pltpu.VMEM(own["pair"].shape, bf16),
            pltpu.VMEM((count, len(edges[0]), 2, tile, HEAD_DIM), bf16),
            pltpu.VMEM((across * (tiles + 2) * tile, HEAD_DIM), bf16),
            pltpu.VMEM((across * (tiles + 2) * tile, HEAD_DIM), bf16),
            pltpu.VMEM((count, tokens, HEAD_DIM), bf16),
            pltpu.SemaphoreType.DMA((count, kinds)),
            pltpu.SemaphoreType.DMA((count, len(edges[0]))),
        ]
    if sides:
        scratch.append(pltpu.VMEM((count, 2, 2, tokens, HEAD_DIM), bf16))
    if corners:
        scratch.append(pltpu.VMEM((count, 2, 2, tile, HEAD_DIM), bf16))
    operands += [x for _, x in given]
    scratch += [pltpu.VMEM(x.shape, bf16) for _, x in given]
    if given:
        scratch.append(pltpu.SemaphoreType.DMA((len(given),)))
    out_type = bf16 if last or not weights else jnp.float32
    if weights:
        operands += list(weights)
        scratch += [
            pltpu.VMEM((depth * HEAD_DIM, width), bf16),
            pltpu.SemaphoreType.DMA((depth, blocks)),
            pltpu.VMEM((tokens, width), out_type),
            pltpu.SemaphoreType.DMA((blocks,)),
        ]
    if total_in is not None:
        operands.append(total_in)
        scratch += [pltpu.VMEM((tokens, width), jnp.float32), pltpu.SemaphoreType.DMA((blocks,))]
    shape = (tokens, width) if weights else (count, tokens, HEAD_DIM)
    return pl.pallas_call(
        kernel,
        out_shape=jax.ShapeDtypeStruct(shape, out_type),
        in_specs=[smem, smem, pl.BlockSpec(memory_space=pltpu.VMEM)] + [anywhere] * len(operands),
        out_specs=anywhere,
        scratch_shapes=scratch,
        compiler_params=pltpu.CompilerParams(vmem_limit_bytes=VMEM_BYTES),
    )(meta, flags, col_masks, *operands)


def on_device(queries, keys, values, out_weight, window_radii, frame_valid):
    _, rows_dev, col_total, width = queries.shape
    heads = width // HEAD_DIM
    tile = ROW_TILE * col_total
    tiles = rows_dev // ROW_TILE
    tokens = tile * tiles
    frame_pairs, height_total = lax.axis_size("frame"), lax.axis_size("height")
    q, k, v = (x.reshape(tokens, width) for x in (queries, keys, values))
    outer_pairs = [(2 * i + 1, 2 * i + 2) for i in range(frame_pairs - 1)]
    outer_pairs += [(target, source) for source, target in outer_pairs]
    swap = [(0, 1), (1, 0)]
    down = [(i, i + 1) for i in range(height_total - 1)]
    up = [(i + 1, i) for i in range(height_total - 1)]
    edge_first = 12
    side_levels = [heads, 14, 12, 10]

    meta, slots, flags, side_level, more_edges, corner_count = plan_heads(
        window_radii, frame_valid, side_levels, edge_first
    )
    order = meta[0]

    col = np.arange(tile) % col_total // COL_TILE
    gap = np.abs(col[:, None] - col[None, :])
    col_masks = jnp.asarray(np.stack([np.where(gap <= x, 0.0, NEG_FILL) for x in range(2)]).astype(np.float32))

    def trade_edges(low, high):
        above, below = lax.ppermute(high, "height", down), lax.ppermute(low, "height", up)
        return above, below, lax.ppermute(above, "head", swap), lax.ppermute(below, "head", swap)

    def rest_of_edges(k, v):
        return trade_edges(*pack_edges(slots, k, v, edge_first, heads - edge_first, tile, tiles))

    def no_edges(k, v):
        return (jnp.zeros((heads - edge_first, 2, tile, HEAD_DIM), k.dtype),) * 4

    def trade_corners(beyond):
        return (
            lax.ppermute(beyond[:, :, tokens - tile :], "height", down),
            lax.ppermute(beyond[:, :, :tile], "height", up),
        )

    def no_corners(beyond):
        return (jnp.zeros((beyond.shape[0], 2, tile, HEAD_DIM), beyond.dtype),) * 2

    def finish(side_count):
        def call(q, k, v, out_weight):
            size = side_count - 4
            parts = [(0, size), (size, 4)]
            rest = heads - side_count
            *packed, low, high = pack_heads(
                order, (k, v), [(*x, (0, 1)) for x in parts], tile, tiles, slots, edge_first
            )
            beyond = [lax.ppermute(x, GRID_AXES, outer_pairs) for x in packed]
            beside = [lax.ppermute(x, "head", swap) for x in packed]
            other_weight = lax.ppermute(out_weight, "head", swap)
            weights = (out_weight, other_weight)
            q, k, v, low, high = lax.optimization_barrier((q, k, v, low, high))
            edges = [trade_edges(low, high)]
            groups = [(*x, (0,)) for x in parts]
            groups += [(side_count, rest, (0,)), (side_count, rest, (1, 2))] if rest else []
            ordered = pack_heads(order, (q, k, v), groups, tile, tiles)
            edges.append(lax.cond(more_edges[0] > 0, rest_of_edges, no_edges, k, v))
            ordered, edges = lax.optimization_barrier((ordered, edges))
            common = (meta, flags, col_masks)
            total = None
            near = beyond[0]
            if rest:
                own = {"query": ordered[2], "pair": ordered[3], "edges": [x[:2] for x in edges]}
                shared = chunk(*common, side_count, own, [], (), None, False, 1024, tile, tiles)
                near, shared = lax.optimization_barrier((near, shared))
            corners = trade_corners(near)
            if rest:
                total = chunk(*common, 0, None, [(side_count, shared)], weights, None, False, 1024, tile, tiles)
                corners, total = lax.optimization_barrier((corners, total))
            own = {"query": ordered[0], "pair": packed[0], "sides": (beside[0], near), "edges": edges, "corners": corners}
            shared = chunk(*common, 0, own, [], (), None, False, 1024, tile, tiles, 4)
            far, shared = lax.optimization_barrier((beyond[1], shared))
            corners = lax.cond(corner_count[0] > size, trade_corners, no_corners, far)
            own = {"query": ordered[1], "pair": packed[1], "sides": (beside[1], far), "edges": edges, "corners": corners}
            total = chunk(*common, size, own, [(0, shared)], weights, total, True, 1024, tile, tiles)
            return total

        return call

    projected = lax.switch(side_level[0], [finish(x) for x in side_levels], q, k, v, out_weight)
    return projected.reshape(1, rows_dev, col_total, out_weight.shape[1])


def solution(mesh):
    return jax.shard_map(
        on_device,
        mesh=mesh,
        in_specs=(
            P(("frame", "head"), "height", None, None),
            P(("frame", "head"), "height", None, None),
            P(("frame", "head"), "height", None, None),
            P("head", None),
            P(),
            P(),
        ),
        out_specs=P(("frame", "head"), "height", None, None),
        check_vma=False,
    )
```

```python
import functools
import math

import jax
import jax.numpy as jnp
import numpy as np
from jax import lax
from jax.experimental import pallas as pl
from jax.experimental.pallas import tpu as pltpu
from jax.sharding import PartitionSpec as P

HEAD_DIM = 128
ROW_TILE = 2
COL_TILE = 16
NEG_FILL = -1e30
GRID_AXES = ("frame", "head")
VMEM_BYTES = 62 * 1024 * 1024
SCALE = HEAD_DIM ** -0.5 * math.log2(math.e)


def plan_heads(window_radii, frame_valid, levels):
    heads = window_radii.shape[0]
    frames = frame_valid.shape[0]

    def kernel(radii_ref, valid_ref, meta_ref, slot_ref, flag_ref, level_ref):
        both, side, edge = (jnp.int32(0) for _ in range(3))
        for head in range(heads):
            rad_f, rad_r = radii_ref[head, 0], radii_ref[head, 1]
            both += rad_f * rad_r
            side += rad_f * (1 - rad_r)
            edge += (1 - rad_f) * rad_r
        starts = [both + side + edge, both + side, both, 0]
        for head in range(heads):
            rad_f, rad_r = radii_ref[head, 0], radii_ref[head, 1]
            kind = 2 * rad_f + rad_r
            place = sum(jnp.where(kind == i, starts[i], 0) for i in range(4))
            slot = place + jnp.where(kind == 2, edge, 0) - jnp.where(kind == 1, side, 0)
            starts = [starts[i] + (kind == i).astype(jnp.int32) for i in range(4)]
            meta_ref[0, place] = head
            meta_ref[1, place] = rad_f
            meta_ref[2, place] = rad_r
            meta_ref[3, place] = radii_ref[head, 2]
            meta_ref[4, place] = slot
            meta_ref[5, place] = head // (heads // 2)
            meta_ref[6, place] = head % (heads // 2)
            slot_ref[slot] = head
        part = lax.axis_index("head")
        frame = 2 * lax.axis_index("frame") + part
        height = lax.axis_index("height")
        inner, outer = frame + 1 - 2 * part, frame - 1 + 2 * part
        outer_ok = (outer >= 0) & (outer < frames) & (valid_ref[jnp.clip(outer, 0, frames - 1)] == 1)
        flag_ref[0] = (valid_ref[inner] == 1).astype(jnp.int32)
        flag_ref[1] = outer_ok.astype(jnp.int32)
        flag_ref[2] = (height > 0).astype(jnp.int32)
        flag_ref[3] = (height < lax.axis_size("height") - 1).astype(jnp.int32)
        flag_ref[4] = part
        level = jnp.int32(0)
        for i, (most_side, most_both, most_edge) in enumerate(levels):
            fits = (both + side <= most_side) & (both <= most_both) & (both + edge <= most_edge)
            level = jnp.where(fits, i, level)
        level_ref[0] = level

    smem = pl.BlockSpec(memory_space=pltpu.SMEM)
    shapes = [(8, heads), (heads,), (8,), (1,)]
    return pl.pallas_call(
        kernel,
        out_shape=[jax.ShapeDtypeStruct(shape, jnp.int32) for shape in shapes],
        in_specs=[smem, smem],
        out_specs=[smem] * len(shapes),
    )(window_radii, frame_valid)


def pack_heads(order, sources, groups, tile, tiles, slots=None, edge_groups=()):
    tokens, width = sources[0].shape
    scalars = [order] if slots is None else [order, slots]
    edge_shapes = [(count, len(sources), tile, HEAD_DIM) for _, count in edge_groups]

    def kernel(*refs):
        order_ref, refs = refs[0], refs[len(scalars) - 1 :]
        slot_ref, refs = refs[0], refs[1:]
        ins, outs = refs[: len(sources)], refs[len(sources) :]

        def gather(from_ref, first, count, which, out):
            def copy(at, carry):
                columns = pl.ds(pl.multiple_of(from_ref[first + at] * HEAD_DIM, HEAD_DIM), HEAD_DIM)
                for index, source in enumerate(which):
                    out[at, index] = ins[source][:, columns]
                return carry

            lax.fori_loop(0, count, copy, 0, unroll=2)

        for (first, count, which), out in zip(groups, outs):
            gather(order_ref, first, count, which, out)
        if slots is not None:
            for i, at in enumerate((0, tiles - 1)):

                @pl.when(pl.program_id(0) == at)
                def _():
                    for j, (first, count) in enumerate(edge_groups):
                        gather(slot_ref, first, count, range(len(sources)), outs[len(groups) + 2 * j + i])

    in_spec = pl.BlockSpec((tile, width), lambda step, *refs: (step, 0))
    out_specs = [
        pl.BlockSpec((count, len(which), tile, HEAD_DIM), lambda step, *refs: (0, 0, step, 0))
        for _, count, which in groups
    ]
    shapes = [(count, len(which), tokens, HEAD_DIM) for _, count, which in groups]
    if slots is not None:
        for shape in edge_shapes:
            out_specs += [pl.BlockSpec(shape, lambda step, *refs: (0, 0, 0, 0))] * 2
            shapes += [shape] * 2
    return pl.pallas_call(
        kernel,
        out_shape=[jax.ShapeDtypeStruct(shape, sources[0].dtype) for shape in shapes],
        grid_spec=pltpu.PrefetchScalarGridSpec(
            num_scalar_prefetch=len(scalars),
            grid=(tiles,),
            in_specs=[in_spec] * len(sources),
            out_specs=out_specs,
        ),
        compiler_params=pltpu.CompilerParams(vmem_limit_bytes=VMEM_BYTES),
    )(*scalars, *sources)


def attend(query, keys, values, col_mask, biases, flip):
    scores = lax.dot_general(
        keys, query, (((1,), (1,)), ((), ())), preferred_element_type=jnp.float32
    )
    mask = jnp.concatenate([col_mask if x is None else col_mask + x for x in biases], axis=0)
    scores = scores * SCALE + mask
    expo = jnp.exp2(scores - jnp.max(scores, axis=0, keepdims=True))
    probs = (expo * (1.0 / jnp.sum(expo, axis=0, keepdims=True))).astype(jnp.bfloat16)
    left, right = (values, probs) if flip else (probs, values)
    out = lax.dot_general(left, right, (((0,), (0,)), ((), ())), preferred_element_type=jnp.float32)
    return (out.T if flip else out).astype(jnp.bfloat16)


def chunk(meta, flags, col_masks, first, own, given, weights, block, tile, tiles, unroll=2):
    tokens = tile * tiles
    count = own["query"].shape[0]
    sides, corners, edges = own.get("sides", ()), own.get("corners", ()), own["edges"]
    places = [(start + i, g, i) for g, (start, x) in enumerate(given) for i in range(x.shape[0])]
    depth = weights[0].shape[0] if weights else 0
    width = weights[0].shape[1] if weights else 0
    blocks = width // block
    across = 1 + len(sides)

    def kernel(meta_ref, flag_ref, mask_ref, *refs):
        refs = list(refs)

        def take(items):
            return [refs.pop(0) for _ in items]

        query_ref, pair_ref = take(range(2))
        side_refs, corner_refs = take(sides), take(corners)
        edge_refs = take(edges)
        given_refs, weight_refs = take(given), take(weights)
        out_ref = refs.pop(0)
        query_buf, pair_buf, edge_buf, key_buf, value_buf, attended, own_sem, edge_sem = take(range(8))
        side_buf, corner_buf = take(sides[:1]), take(corners[:1])
        if weights:
            given_sem, weight_buf, weight_sem, out_buf, out_sem = take(range(5))

        def own_copies(at):
            pairs = [(query_ref.at[at], query_buf.at[at]), (pair_ref.at[at], pair_buf.at[at])]
            pairs += [(x.at[at], side_buf[0].at[at, i]) for i, x in enumerate(side_refs)]
            pairs += [(x.at[at], corner_buf[0].at[at, i]) for i, x in enumerate(corner_refs)]
            return [pltpu.make_async_copy(x, y, own_sem.at[at, i]) for i, (x, y) in enumerate(pairs)]

        def edge_copies(at, slot):
            return [
                pltpu.make_async_copy(x.at[slot], edge_buf.at[at, i], edge_sem.at[at, i])
                for i, x in enumerate(edge_refs)
            ]

        def begin_own(at, carry):
            for copy in own_copies(at):
                copy.start()
            slot = meta_ref[4, first + at]

            for copy in edge_copies(at, jnp.minimum(slot, edges[0].shape[0] - 1)):
                copy.start()

            return carry

        def head_columns(place):
            half = jnp.where(meta_ref[5, place] == flag_ref[4], 0, depth)
            return pl.ds(pl.multiple_of(half + meta_ref[6, place] * HEAD_DIM, HEAD_DIM), HEAD_DIM)

        def given_copy(index):
            place, g, i = places[index]
            return pltpu.make_async_copy(
                given_refs[g].at[i], attended.at[:, head_columns(place)], given_sem.at[index]
            )

        def columns(at):
            return pl.ds(pl.multiple_of(at * block, block), block)

        def weight_copies(at):
            return [
                pltpu.make_async_copy(x.at[:, columns(at)], weight_buf.at[i, :, columns(at)], weight_sem.at[i, at])
                for i, x in enumerate(weight_refs)
            ]

        def out_copy(at):
            return pltpu.make_async_copy(out_buf.at[:, columns(at)], out_ref.at[:, columns(at)], out_sem.at[at])

        def begin_share(at, carry):
            for copy in weight_copies(at):
                copy.start()
            return carry

        def tile_rows(at, size=1):
            return pl.ds(pl.multiple_of(at * tile, tile), size * tile)

        def off(ok):
            return jnp.where(ok, 0.0, NEG_FILL)

        def lay(row, source_k, source_v):
            key_buf[tile_rows(row), :] = source_k
            value_buf[tile_rows(row), :] = source_v

        def head_step(head, carry):
            place = first + head
            rad_f, rad_r, rad_c = meta_ref[1, place], meta_ref[2, place], meta_ref[3, place]
            for copy in own_copies(head) + edge_copies(head, 0):
                copy.wait()
            col_mask = mask_ref[rad_c]
            side_bias = [None] + [off((rad_f > 0) & (flag_ref[i] != 0)) for i in range(across - 1)]
            bodies = [pair_buf.at[head]] + [side_buf[0].at[head, i] for i in range(across - 1)]

            def band_bias(at):
                low = off((rad_r > 0) & ((at > 0) | (flag_ref[2] != 0)))
                high = off((rad_r > 0) & ((at < tiles - 1) | (flag_ref[3] != 0)))
                return low, None, high

            def run(at, start, biases, flip):
                rows, held = tile_rows(at), tile_rows(start, len(biases))
                found = attend(
                    query_buf[head, 0, rows, :], key_buf[held, :], value_buf[held, :], col_mask, biases, flip
                )
                if weights:
                    attended[rows, head_columns(place)] = found
                else:
                    attended[head, rows, :] = found

            def fill(band):
                def step(at, carry):
                    rows = tile_rows(at)
                    for which, body in enumerate(bodies):
                        lay(across * (at + band) + which, body[0, rows, :], body[1, rows, :])
                    return carry

                lax.fori_loop(0, tiles, step, 0, unroll=2)

            def with_rows():
                ends = [(edge_buf.at[head, 2 * i], edge_buf.at[head, 2 * i + 1]) for i in range(len(edges) // 2)]
                if corners:
                    ends.append((corner_buf[0].at[head, 0], corner_buf[0].at[head, 1]))
                for which, (low, high) in enumerate(ends):
                    lay(which, low[0], low[1])
                    lay(across * (tiles + 1) + which, high[0], high[1])
                fill(1)

                def each(at, carry):
                    biases = []
                    for x in band_bias(at):
                        for y in side_bias:
                            biases.append(x if y is None else y if x is None else jnp.minimum(x, y))
                    run(at, across * at, biases, across > 1)
                    return carry

                lax.fori_loop(0, tiles, each, 0, unroll=tiles if across == 1 else unroll)

            if sides:
                pl.when(rad_r > 0)(with_rows)

                @pl.when(rad_r == 0)
                def _():
                    fill(0)

                    def each(at, carry):
                        run(at, across * at, side_bias, False)
                        return carry

                    lax.fori_loop(0, tiles, each, 0, unroll=tiles)

            else:
                with_rows()
            return carry

        def share(at, carry):
            for copy in weight_copies(at):
                copy.wait()
            total = sum(
                jnp.dot(
                    attended[:, i * depth : (i + 1) * depth], weight_buf[i, :, columns(at)],
                    preferred_element_type=jnp.float32,
                )
                for i in range(2)
            )
            out_buf[:, columns(at)] = total.astype(out_buf.dtype)
            out_copy(at).start()
            return carry

        def end_share(at, carry):
            out_copy(at).wait()
            return carry

        lax.fori_loop(0, count, begin_own, 0)
        if weights:
            for index in range(len(places)):
                given_copy(index).start()
            lax.fori_loop(0, blocks, begin_share, 0)
        lax.fori_loop(0, count, head_step, 0)
        if weights:
            for index in range(len(places)):
                given_copy(index).wait()
        if weights:
            lax.fori_loop(0, blocks, share, 0)
            lax.fori_loop(0, blocks, end_share, 0)
        else:
            done = pltpu.make_async_copy(attended, out_ref, own_sem.at[0, 0])
            done.start()
            done.wait()

    anywhere, smem = pl.BlockSpec(memory_space=pl.ANY), pl.BlockSpec(memory_space=pltpu.SMEM)
    operands, scratch = [], []
    bf16 = jnp.bfloat16
    operands += [own["query"], own["pair"], *sides, *corners, *edges]
    kinds = 2 + len(sides) + len(corners)
    scratch += [
            pltpu.VMEM(own["query"].shape, bf16),
            pltpu.VMEM(own["pair"].shape, bf16),
            pltpu.VMEM((count, len(edges), 2, tile, HEAD_DIM), bf16),
            pltpu.VMEM((across * (tiles + 2) * tile, HEAD_DIM), bf16),
            pltpu.VMEM((across * (tiles + 2) * tile, HEAD_DIM), bf16),
            pltpu.VMEM((tokens, 2 * depth) if weights else (count, tokens, HEAD_DIM), bf16),
            pltpu.SemaphoreType.DMA((count, kinds)),
            pltpu.SemaphoreType.DMA((count, len(edges))),
        ]
    if sides:
        scratch.append(pltpu.VMEM((count, 2, 2, tokens, HEAD_DIM), bf16))
    if corners:
        scratch.append(pltpu.VMEM((count, 2, 2, tile, HEAD_DIM), bf16))
    operands += [x for _, x in given]
    out_type = bf16
    if weights:
        operands += list(weights)
        scratch += [
            pltpu.SemaphoreType.DMA((len(places),)),
            pltpu.VMEM((2, depth, width), bf16),
            pltpu.SemaphoreType.DMA((2, blocks)),
            pltpu.VMEM((tokens, width), out_type),
            pltpu.SemaphoreType.DMA((blocks,)),
        ]
    shape = (tokens, width) if weights else (count, tokens, HEAD_DIM)
    return pl.pallas_call(
        kernel,
        out_shape=jax.ShapeDtypeStruct(shape, out_type),
        in_specs=[smem, smem, pl.BlockSpec(memory_space=pltpu.VMEM)] + [anywhere] * len(operands),
        out_specs=anywhere,
        scratch_shapes=scratch,
        compiler_params=pltpu.CompilerParams(vmem_limit_bytes=VMEM_BYTES),
    )(meta, flags, col_masks, *operands)


def on_device(queries, keys, values, out_weight, window_radii, frame_valid):
    _, rows_dev, col_total, width = queries.shape
    heads = width // HEAD_DIM
    tile = ROW_TILE * col_total
    tiles = rows_dev // ROW_TILE
    tokens = tile * tiles
    frame_pairs, height_total = lax.axis_size("frame"), lax.axis_size("height")
    q, k, v = (x.reshape(tokens, width) for x in (queries, keys, values))
    outer_pairs = [(2 * i + 1, 2 * i + 2) for i in range(frame_pairs - 1)]
    outer_pairs += [(target, source) for source, target in outer_pairs]
    swap = [(0, 1), (1, 0)]
    down = [(i, i + 1) for i in range(height_total - 1)]
    up = [(i + 1, i) for i in range(height_total - 1)]
    levels = [(heads, heads, heads), (16, 10, 16), (13, 8, 14), (10, 6, 12)]

    meta, slots, flags, level = plan_heads(window_radii, frame_valid, levels)
    order = meta[0]

    col = np.arange(tile) % col_total // COL_TILE
    gap = np.abs(col[:, None] - col[None, :])
    col_masks = jnp.asarray(np.stack([np.where(gap <= x, 0.0, NEG_FILL) for x in range(2)]).astype(np.float32))

    def trade_edges(low, high):
        return lax.ppermute(high, "height", down), lax.ppermute(low, "height", up)

    def to_sibling(pair):
        return tuple(lax.ppermute(x, "head", swap) for x in pair)

    def trade_corners(beyond):
        return (
            lax.ppermute(beyond[:, :, tokens - tile :], "height", down),
            lax.ppermute(beyond[:, :, :tile], "height", up),
        )

    def finish(side_count, both_count, edge_count):
        def call(q, k, v, out_weight):
            size = both_count if both_count < side_count else side_count // 2
            parts = [(0, size), (size, side_count - size)]
            rest = heads - side_count
            *packed, low, high = pack_heads(
                order, (k, v), [(*x, (0, 1)) for x in parts], tile, tiles, slots, [(0, edge_count)]
            )
            beyond = [lax.ppermute(x, GRID_AXES, outer_pairs) for x in packed]
            beside = [lax.ppermute(x, "head", swap) for x in packed]
            weights = (out_weight, lax.ppermute(out_weight, "head", swap))
            edges = trade_edges(low, high)
            groups = [(*x, (0,)) for x in parts]
            groups += [(side_count, rest, (0,)), (side_count, rest, (1, 2))] if rest else []
            ordered = pack_heads(order, (q, k, v), groups, tile, tiles)
            edges, ordered = lax.optimization_barrier((edges, ordered))
            edges += to_sibling(edges)
            edges, ordered = lax.optimization_barrier((edges, ordered))
            common = (meta, flags, col_masks)
            shared = []
            near = beyond[0]
            if rest:
                own = {"query": ordered[2], "pair": ordered[3], "edges": edges[:2]}
                lone = chunk(*common, side_count, own, [], (), 1024, tile, tiles)
                near, lone = lax.optimization_barrier((near, lone))
                shared.append((side_count, lone))
            corners = trade_corners(near)
            own = {"query": ordered[0], "pair": packed[0], "sides": (beside[0], near), "edges": edges, "corners": corners}
            first = chunk(*common, 0, own, [], (), 1024, tile, tiles, 4)
            far, first = lax.optimization_barrier((beyond[1], first))
            shared.append((0, first))
            if both_count > size:
                corners = trade_corners(far)
            own = {"query": ordered[1], "pair": packed[1], "sides": (beside[1], far), "edges": edges, "corners": corners}
            return chunk(*common, size, own, shared, weights, 1024, tile, tiles)

        return call

    projected = lax.switch(level[0], [finish(*x) for x in levels], q, k, v, out_weight)
    return projected.reshape(1, rows_dev, col_total, out_weight.shape[1])


def solution(mesh):
    return jax.shard_map(
        on_device,
        mesh=mesh,
        in_specs=(
            P(("frame", "head"), "height", None, None),
            P(("frame", "head"), "height", None, None),
            P(("frame", "head"), "height", None, None),
            P("head", None),
            P(),
            P(),
        ),
        out_specs=P(("frame", "head"), "height", None, None),
        check_vma=False,
    )
```

```python
import functools
import math

import jax
import jax.numpy as jnp
import numpy as np
from jax import lax
from jax.experimental import pallas as pl
from jax.experimental.pallas import tpu as pltpu
from jax.sharding import PartitionSpec as P

HEAD_DIM = 128
ROW_TILE = 2
COL_TILE = 16
NEG_FILL = -1e30
GRID_AXES = ("frame", "head")
VMEM_BYTES = 62 * 1024 * 1024
SCALE = HEAD_DIM ** -0.5 * math.log2(math.e)


def plan_heads(window_radii, frame_valid, levels):
    heads = window_radii.shape[0]
    frames = frame_valid.shape[0]

    def kernel(radii_ref, valid_ref, meta_ref, slot_ref, flag_ref, level_ref):
        both, side, edge = (jnp.int32(0) for _ in range(3))
        for head in range(heads):
            rad_f, rad_r = radii_ref[head, 0], radii_ref[head, 1]
            both += rad_f * rad_r
            side += rad_f * (1 - rad_r)
            edge += (1 - rad_f) * rad_r
        starts = [both + side, heads - edge, both, 0]
        for head in range(heads):
            rad_f, rad_r = radii_ref[head, 0], radii_ref[head, 1]
            kind = 2 * rad_f + rad_r
            place = sum(jnp.where(kind == i, starts[i], 0) for i in range(4))
            slot = place + jnp.where(kind == 1, both - (heads - edge), jnp.where(kind == 3, 0, edge))
            starts = [starts[i] + (kind == i).astype(jnp.int32) for i in range(4)]
            meta_ref[0, place] = head
            meta_ref[1, place] = rad_f
            meta_ref[2, place] = rad_r
            meta_ref[3, place] = radii_ref[head, 2]
            meta_ref[4, place] = slot
            meta_ref[5, place] = head // (heads // 2)
            meta_ref[6, place] = head % (heads // 2)
            slot_ref[slot] = head
        part = lax.axis_index("head")
        frame = 2 * lax.axis_index("frame") + part
        height = lax.axis_index("height")
        inner, outer = frame + 1 - 2 * part, frame - 1 + 2 * part
        outer_ok = (outer >= 0) & (outer < frames) & (valid_ref[jnp.clip(outer, 0, frames - 1)] == 1)
        flag_ref[0] = (valid_ref[inner] == 1).astype(jnp.int32)
        flag_ref[1] = outer_ok.astype(jnp.int32)
        flag_ref[2] = (height > 0).astype(jnp.int32)
        flag_ref[3] = (height < lax.axis_size("height") - 1).astype(jnp.int32)
        flag_ref[4] = part
        level = jnp.int32(0)
        for i, (most_side, most_both, most_edge) in enumerate(levels):
            fits = (both + side <= most_side) & (both <= most_both) & (both + edge <= most_edge)
            fits = fits & ((edge <= heads - most_side) | (most_side == heads))
            level = jnp.where(fits, i, level)
        level_ref[0] = level

    smem = pl.BlockSpec(memory_space=pltpu.SMEM)
    shapes = [(8, heads), (heads,), (8,), (1,)]
    return pl.pallas_call(
        kernel,
        out_shape=[jax.ShapeDtypeStruct(shape, jnp.int32) for shape in shapes],
        in_specs=[smem, smem],
        out_specs=[smem] * len(shapes),
    )(window_radii, frame_valid)


def pack_heads(order, sources, groups, tile, tiles, slots=None, edge_groups=()):
    tokens, width = sources[0].shape
    scalars = [order] if slots is None else [order, slots]
    edge_shapes = [(count, len(sources), tile, HEAD_DIM) for _, count in edge_groups]

    def kernel(*refs):
        order_ref, refs = refs[0], refs[len(scalars) - 1 :]
        slot_ref, refs = refs[0], refs[1:]
        ins, outs = refs[: len(sources)], refs[len(sources) :]

        def gather(from_ref, first, count, which, out):
            def copy(at, carry):
                columns = pl.ds(pl.multiple_of(from_ref[first + at] * HEAD_DIM, HEAD_DIM), HEAD_DIM)
                for index, source in enumerate(which):
                    out[at, index] = ins[source][:, columns]
                return carry

            lax.fori_loop(0, count, copy, 0, unroll=2)

        for (first, count, which), out in zip(groups, outs):
            gather(order_ref, first, count, which, out)
        if slots is not None:
            for i, at in enumerate((0, tiles - 1)):

                @pl.when(pl.program_id(0) == at)
                def _():
                    for j, (first, count) in enumerate(edge_groups):
                        gather(slot_ref, first, count, range(len(sources)), outs[len(groups) + 2 * j + i])

    in_spec = pl.BlockSpec((tile, width), lambda step, *refs: (step, 0))
    out_specs = [
        pl.BlockSpec((count, len(which), tile, HEAD_DIM), lambda step, *refs: (0, 0, step, 0))
        for _, count, which in groups
    ]
    shapes = [(count, len(which), tokens, HEAD_DIM) for _, count, which in groups]
    if slots is not None:
        for shape in edge_shapes:
            out_specs += [pl.BlockSpec(shape, lambda step, *refs: (0, 0, 0, 0))] * 2
            shapes += [shape] * 2
    return pl.pallas_call(
        kernel,
        out_shape=[jax.ShapeDtypeStruct(shape, sources[0].dtype) for shape in shapes],
        grid_spec=pltpu.PrefetchScalarGridSpec(
            num_scalar_prefetch=len(scalars),
            grid=(tiles,),
            in_specs=[in_spec] * len(sources),
            out_specs=out_specs,
        ),
        compiler_params=pltpu.CompilerParams(vmem_limit_bytes=VMEM_BYTES),
    )(*scalars, *sources)


def attend(query, keys, values, col_mask, biases, flip):
    scores = lax.dot_general(
        keys, query, (((1,), (1,)), ((), ())), preferred_element_type=jnp.float32
    )
    mask = jnp.concatenate([col_mask if x is None else col_mask + x for x in biases], axis=0)
    scores = scores * SCALE + mask
    expo = jnp.exp2(scores - jnp.max(scores, axis=0, keepdims=True))
    probs = (expo * (1.0 / jnp.sum(expo, axis=0, keepdims=True))).astype(jnp.bfloat16)
    left, right = (values, probs) if flip else (probs, values)
    out = lax.dot_general(left, right, (((0,), (0,)), ((), ())), preferred_element_type=jnp.float32)
    return (out.T if flip else out).astype(jnp.bfloat16)


def chunk(meta, flags, col_masks, first, own, given, weights, total_in, last, tile, tiles, unroll=2):
    tokens = tile * tiles
    count = own["query"].shape[0] if own else 0
    sides, corners = (own.get("sides", ()), own.get("corners", ())) if own else ((), ())
    edges = own["edges"] if own else ()
    places = [(start + i, g, i) for g, (start, x) in enumerate(given) for i in range(x.shape[0])]
    places += [(first + i, None, i) for i in range(count)]
    depth = len(places)
    width = weights[0].shape[1] if weights else 0
    blocks, parts = 4, 2
    block, part_width = width // blocks, width // parts
    across = 1 + len(sides)

    def kernel(meta_ref, flag_ref, mask_ref, *refs):
        refs = list(refs)

        def take(items):
            return [refs.pop(0) for _ in items]

        query_ref, pair_ref = take(range(2)) if own else (None, None)
        side_refs, corner_refs = take(sides), take(corners)
        edge_refs = take(edges)
        given_refs, weight_refs = take(given), take(weights)
        total_ref = refs.pop(0) if total_in is not None else None
        out_ref = refs.pop(0)
        if own:
            query_buf, pair_buf, edge_buf, key_buf, value_buf, attended, own_sem, edge_sem = take(range(8))
        side_buf, corner_buf = take(sides[:1]), take(corners[:1])
        given_bufs = take(given)
        if given:
            given_sem = refs.pop(0)
        if weights:
            weight_buf, weight_sem, out_buf, out_sem = take(range(4))
        if total_ref is not None:
            total_buf, total_sem = take(range(2))

        def own_copies(at):
            pairs = [(query_ref.at[at], query_buf.at[at]), (pair_ref.at[at], pair_buf.at[at])]
            pairs += [(x.at[at], side_buf[0].at[at, i]) for i, x in enumerate(side_refs)]
            pairs += [(x.at[at], corner_buf[0].at[at, i]) for i, x in enumerate(corner_refs)]
            return [pltpu.make_async_copy(x, y, own_sem.at[at, i]) for i, (x, y) in enumerate(pairs)]

        def edge_copies(at, slot):
            return [
                pltpu.make_async_copy(x.at[slot], edge_buf.at[at, i], edge_sem.at[at, i])
                for i, x in enumerate(edge_refs)
            ]

        def begin_own(at, carry):
            for copy in own_copies(at):
                copy.start()
            slot = meta_ref[4, first + at]

            if edges:
                for copy in edge_copies(at, jnp.minimum(slot, edges[0].shape[0] - 1)):
                    copy.start()

            return carry

        def given_copy(g):
            return pltpu.make_async_copy(given_refs[g], given_bufs[g], given_sem.at[g])

        def columns(at):
            return pl.ds(pl.multiple_of(at * block, block), block)

        def weight_copy(index, part, source):
            row = pl.multiple_of(meta_ref[6, places[index][0]] * HEAD_DIM, HEAD_DIM)
            wide = pl.ds(pl.multiple_of(part * part_width, part_width), part_width)
            return pltpu.make_async_copy(
                source.at[pl.ds(row, HEAD_DIM), wide],
                weight_buf.at[pl.ds(index * HEAD_DIM, HEAD_DIM), wide],
                weight_sem.at[index, part],
            )

        def total_copy(at):
            return pltpu.make_async_copy(total_ref.at[:, columns(at)], total_buf.at[:, columns(at)], total_sem.at[at])

        def out_copy(at):
            return pltpu.make_async_copy(out_buf.at[:, columns(at)], out_ref.at[:, columns(at)], out_sem.at[at])

        def begin_share(part, carry):
            for index in range(depth):
                mine = meta_ref[5, places[index][0]] == flag_ref[4]

                @pl.when(mine)
                def _():
                    weight_copy(index, part, weight_refs[0]).start()

                @pl.when(jnp.logical_not(mine))
                def _():
                    weight_copy(index, part, weight_refs[1]).start()

            if total_ref is not None:
                for at in range(blocks // parts):
                    total_copy(part * (blocks // parts) + at).start()
            return carry

        def tile_rows(at, size=1):
            return pl.ds(pl.multiple_of(at * tile, tile), size * tile)

        def off(ok):
            return jnp.where(ok, 0.0, NEG_FILL)

        def lay(row, source_k, source_v):
            key_buf[tile_rows(row), :] = source_k
            value_buf[tile_rows(row), :] = source_v

        def head_step(head, carry):
            place = first + head
            rad_f, rad_r, rad_c = meta_ref[1, place], meta_ref[2, place], meta_ref[3, place]
            for copy in own_copies(head) + edge_copies(head, 0):
                copy.wait()
            col_mask = mask_ref[rad_c]
            side_bias = [None] + [off((rad_f > 0) & (flag_ref[i] != 0)) for i in range(across - 1)]
            bodies = [pair_buf.at[head]] + [side_buf[0].at[head, i] for i in range(across - 1)]

            def band_bias(at):
                low = off((rad_r > 0) & ((at > 0) | (flag_ref[2] != 0)))
                high = off((rad_r > 0) & ((at < tiles - 1) | (flag_ref[3] != 0)))
                return low, None, high

            def run(at, start, biases, flip):
                rows, held = tile_rows(at), tile_rows(start, len(biases))
                attended[head, rows, :] = attend(
                    query_buf[head, 0, rows, :], key_buf[held, :], value_buf[held, :], col_mask, biases, flip
                )

            def fill(band):
                def step(at, carry):
                    rows = tile_rows(at)
                    for which, body in enumerate(bodies):
                        lay(across * (at + band) + which, body[0, rows, :], body[1, rows, :])
                    return carry

                lax.fori_loop(0, tiles, step, 0, unroll=2)

            def with_rows():
                ends = [(edge_buf.at[head, 2 * i], edge_buf.at[head, 2 * i + 1]) for i in range(len(edges) // 2)]
                if corners:
                    ends.append((corner_buf[0].at[head, 0], corner_buf[0].at[head, 1]))
                for which, (low, high) in enumerate(ends):
                    lay(which, low[0], low[1])
                    lay(across * (tiles + 1) + which, high[0], high[1])
                fill(1)

                def each(at, carry):
                    biases = []
                    for x in band_bias(at):
                        for y in side_bias:
                            biases.append(x if y is None else y if x is None else jnp.minimum(x, y))
                    run(at, across * at, biases, across > 1)
                    return carry

                lax.fori_loop(0, tiles, each, 0, unroll=tiles if across == 1 else unroll)

            if sides:
                if edges:
                    pl.when(rad_r > 0)(with_rows)

                @pl.when((rad_r == 0) if edges else True)
                def _():
                    fill(0)

                    def each(at, carry):
                        run(at, across * at, side_bias, False)
                        return carry

                    lax.fori_loop(0, tiles, each, 0, unroll=tiles)

            else:
                with_rows()
            return carry

        def share(part, carry):
            for index in range(depth):
                weight_copy(index, part, weight_refs[0]).wait()

            def each(i, carry):
                at = part * (blocks // parts) + i
                held = [attended[i] if g is None else given_bufs[g][i] for _, g, i in places]
                left = jnp.concatenate(held, axis=1)
                total = jnp.dot(left, weight_buf[:, columns(at)], preferred_element_type=jnp.float32)
                if total_ref is not None:
                    total_copy(at).wait()
                    total += total_buf[:, columns(at)]
                out_buf[:, columns(at)] = total.astype(out_buf.dtype)
                out_copy(at).start()
                return carry

            return lax.fori_loop(0, blocks // parts, each, carry)

        def end_share(at, carry):
            out_copy(at).wait()
            return carry

        if own:
            lax.fori_loop(0, count, begin_own, 0)
        for g in range(len(given)):
            given_copy(g).start()
        if weights:
            lax.fori_loop(0, parts, begin_share, 0)
        if own:
            lax.fori_loop(0, count, head_step, 0)
        for g in range(len(given)):
            given_copy(g).wait()
        if weights:
            lax.fori_loop(0, parts, share, 0)
            lax.fori_loop(0, blocks, end_share, 0)
        else:
            done = pltpu.make_async_copy(attended, out_ref, own_sem.at[0, 0])
            done.start()
            done.wait()

    anywhere, smem = pl.BlockSpec(memory_space=pl.ANY), pl.BlockSpec(memory_space=pltpu.SMEM)
    operands, scratch = [], []
    bf16 = jnp.bfloat16
    if own:
        operands += [own["query"], own["pair"], *sides, *corners, *edges]
        kinds = 2 + len(sides) + len(corners)
        scratch += [
            pltpu.VMEM(own["query"].shape, bf16),
            pltpu.VMEM(own["pair"].shape, bf16),
            pltpu.VMEM((count, max(len(edges), 1), 2, tile, HEAD_DIM), bf16),
            pltpu.VMEM((across * (tiles + 2) * tile, HEAD_DIM), bf16),
            pltpu.VMEM((across * (tiles + 2) * tile, HEAD_DIM), bf16),
            pltpu.VMEM((count, tokens, HEAD_DIM), bf16),
            pltpu.SemaphoreType.DMA((count, kinds)),
            pltpu.SemaphoreType.DMA((count, max(len(edges), 1))),
        ]
    if sides:
        scratch.append(pltpu.VMEM((count, 2, 2, tokens, HEAD_DIM), bf16))
    if corners:
        scratch.append(pltpu.VMEM((count, 2, 2, tile, HEAD_DIM), bf16))
    operands += [x for _, x in given]
    scratch += [pltpu.VMEM(x.shape, bf16) for _, x in given]
    if given:
        scratch.append(pltpu.SemaphoreType.DMA((len(given),)))
    out_type = bf16 if last or not weights else jnp.float32
    if weights:
        operands += list(weights)
        scratch += [
            pltpu.VMEM((depth * HEAD_DIM, width), bf16),
            pltpu.SemaphoreType.DMA((depth, parts)),
            pltpu.VMEM((tokens, width), out_type),
            pltpu.SemaphoreType.DMA((blocks,)),
        ]
    if total_in is not None:
        operands.append(total_in)
        scratch += [pltpu.VMEM((tokens, width), jnp.float32), pltpu.SemaphoreType.DMA((blocks,))]
    shape = (tokens, width) if weights else (count, tokens, HEAD_DIM)
    return pl.pallas_call(
        kernel,
        out_shape=jax.ShapeDtypeStruct(shape, out_type),
        in_specs=[smem, smem, pl.BlockSpec(memory_space=pltpu.VMEM)] + [anywhere] * len(operands),
        out_specs=anywhere,
        scratch_shapes=scratch,
        compiler_params=pltpu.CompilerParams(vmem_limit_bytes=VMEM_BYTES),
    )(meta, flags, col_masks, *operands)


def on_device(queries, keys, values, out_weight, window_radii, frame_valid):
    _, rows_dev, col_total, width = queries.shape
    heads = width // HEAD_DIM
    tile = ROW_TILE * col_total
    tiles = rows_dev // ROW_TILE
    tokens = tile * tiles
    frame_pairs, height_total = lax.axis_size("frame"), lax.axis_size("height")
    q, k, v = (x.reshape(tokens, width) for x in (queries, keys, values))
    outer_pairs = [(2 * i + 1, 2 * i + 2) for i in range(frame_pairs - 1)]
    outer_pairs += [(target, source) for source, target in outer_pairs]
    swap = [(0, 1), (1, 0)]
    down = [(i, i + 1) for i in range(height_total - 1)]
    up = [(i + 1, i) for i in range(height_total - 1)]
    levels = [(heads, heads, heads), (16, 10, 16), (13, 8, 14), (10, 6, 12)]

    meta, slots, flags, level = plan_heads(window_radii, frame_valid, levels)
    order = meta[0]

    col = np.arange(tile) % col_total // COL_TILE
    gap = np.abs(col[:, None] - col[None, :])
    col_masks = jnp.asarray(np.stack([np.where(gap <= x, 0.0, NEG_FILL) for x in range(2)]).astype(np.float32))

    def trade_edges(low, high):
        return lax.ppermute(high, "height", down), lax.ppermute(low, "height", up)

    def to_sibling(pair):
        return tuple(lax.ppermute(x, "head", swap) for x in pair)

    def trade_corners(beyond):
        return (
            lax.ppermute(beyond[:, :, tokens - tile :], "height", down),
            lax.ppermute(beyond[:, :, :tile], "height", up),
        )

    def finish(side_count, both_count, edge_count):
        def call(q, k, v, out_weight):
            size = both_count if both_count < side_count else side_count // 2
            parts = [(0, size), (size, side_count - size)]
            rest = heads - side_count
            *packed, low, high = pack_heads(
                order, (k, v), [(*x, (0, 1)) for x in parts], tile, tiles, slots, [(0, edge_count)]
            )
            beyond = [lax.ppermute(x, GRID_AXES, outer_pairs) for x in packed]
            beside = [lax.ppermute(x, "head", swap) for x in packed]
            weights = (out_weight, lax.ppermute(out_weight, "head", swap))
            edges = trade_edges(low, high)
            groups = [(*x, (0,)) for x in parts]
            groups += [(side_count, rest, (0,)), (side_count, rest, (1, 2))] if rest else []
            ordered = pack_heads(order, (q, k, v), groups, tile, tiles)
            edges, ordered = lax.optimization_barrier((edges, ordered))
            edges += to_sibling(edges)
            edges, ordered = lax.optimization_barrier((edges, ordered))
            common = (meta, flags, col_masks)
            shared = []
            near = beyond[0]
            if rest:
                own = {"query": ordered[2], "pair": ordered[3], "edges": edges[:2]}
                lone = chunk(*common, side_count, own, [], (), None, False, tile, tiles)
                near, lone = lax.optimization_barrier((near, lone))
            corners = trade_corners(near)
            total = None
            if rest:
                total = chunk(*common, 0, None, [(side_count, lone)], weights, None, False, tile, tiles)
                corners, total = lax.optimization_barrier((corners, total))
            own = {"query": ordered[0], "pair": packed[0], "sides": (beside[0], near), "edges": edges, "corners": corners}
            first = chunk(*common, 0, own, [], (), None, False, tile, tiles, 4)
            far, first = lax.optimization_barrier((beyond[1], first))
            shared.append((0, first))
            own = {"query": ordered[1], "pair": packed[1], "sides": (beside[1], far), "edges": ()}
            if both_count > size:
                own.update({"edges": edges, "corners": trade_corners(far)})
            return chunk(*common, size, own, shared, weights, total, True, tile, tiles)

        return call

    projected = lax.switch(level[0], [finish(*x) for x in levels], q, k, v, out_weight)
    return projected.reshape(1, rows_dev, col_total, out_weight.shape[1])


def solution(mesh):
    return jax.shard_map(
        on_device,
        mesh=mesh,
        in_specs=(
            P(("frame", "head"), "height", None, None),
            P(("frame", "head"), "height", None, None),
            P(("frame", "head"), "height", None, None),
            P("head", None),
            P(),
            P(),
        ),
        out_specs=P(("frame", "head"), "height", None, None),
        check_vma=False,
    )
```

```python
import functools
import math

import jax
import jax.numpy as jnp
import numpy as np
from jax import lax
from jax.experimental import pallas as pl
from jax.experimental.pallas import tpu as pltpu
from jax.sharding import PartitionSpec as P

HEAD_DIM = 128
ROW_TILE = 2
COL_TILE = 16
NEG_FILL = -1e30
GRID_AXES = ("frame", "head")
VMEM_BYTES = 62 * 1024 * 1024
SCALE = HEAD_DIM ** -0.5 * math.log2(math.e)


def plan_heads(window_radii, frame_valid, levels):
    heads = window_radii.shape[1]
    frames = frame_valid.shape[0]

    def kernel(radii_ref, valid_ref, meta_ref, slot_ref, flag_ref, level_ref):
        both, side, edge = (jnp.int32(0) for _ in range(3))
        for head in range(heads):
            rad_f, rad_r = radii_ref[0, head], radii_ref[1, head]
            both += rad_f * rad_r
            side += rad_f * (1 - rad_r)
            edge += (1 - rad_f) * rad_r
        starts = [both + side, heads - edge, both, 0]
        for head in range(heads):
            rad_f, rad_r = radii_ref[0, head], radii_ref[1, head]
            kind = 2 * rad_f + rad_r
            place = sum(jnp.where(kind == i, starts[i], 0) for i in range(4))
            slot = place + jnp.where(kind == 1, both - (heads - edge), jnp.where(kind == 3, 0, edge))
            starts = [starts[i] + (kind == i).astype(jnp.int32) for i in range(4)]
            meta_ref[0, place] = head
            meta_ref[1, place] = rad_f
            meta_ref[2, place] = rad_r
            meta_ref[3, place] = radii_ref[2, head]
            meta_ref[4, place] = slot
            meta_ref[5, place] = head // (heads // 2)
            meta_ref[6, place] = head % (heads // 2)
            slot_ref[slot] = head
        part = lax.axis_index("head")
        frame = 2 * lax.axis_index("frame") + part
        height = lax.axis_index("height")
        inner, outer = frame + 1 - 2 * part, frame - 1 + 2 * part
        outer_ok = (outer >= 0) & (outer < frames) & (valid_ref[jnp.clip(outer, 0, frames - 1)] == 1)
        flag_ref[0] = (valid_ref[inner] == 1).astype(jnp.int32)
        flag_ref[1] = outer_ok.astype(jnp.int32)
        flag_ref[2] = (height > 0).astype(jnp.int32)
        flag_ref[3] = (height < lax.axis_size("height") - 1).astype(jnp.int32)
        flag_ref[4] = part
        level = jnp.int32(0)
        for i, (most_side, most_both, most_edge) in enumerate(levels):
            fits = (both + side <= most_side) & (both <= most_both) & (both + edge <= most_edge)
            fits = fits & ((edge <= heads - most_side) | (most_side == heads))
            level = jnp.where(fits, i, level)
        level_ref[0] = level

    smem = pl.BlockSpec(memory_space=pltpu.SMEM)
    shapes = [(8, heads), (heads,), (8,), (1,)]
    return pl.pallas_call(
        kernel,
        out_shape=[jax.ShapeDtypeStruct(shape, jnp.int32) for shape in shapes],
        in_specs=[smem, smem],
        out_specs=[smem] * len(shapes),
    )(window_radii, frame_valid)


def pack_heads(order, sources, groups, tile, tiles, slots=None, edge_groups=()):
    tokens, width = sources[0].shape
    kinds = len(sources)
    scalars = [order] if slots is None else [order, slots]
    shapes = [(count, len(which), tokens, HEAD_DIM) for _, count, which in groups]
    whole = len(shapes)
    shapes += [(count, kinds, tile, HEAD_DIM) for _, count in edge_groups for _ in range(2)]

    def kernel(*refs):
        scalar_refs, refs = refs[: len(scalars)], refs[len(scalars) :]
        ins, refs = refs[:kinds], refs[kinds:]
        outs, refs = refs[: len(shapes)], refs[len(shapes) :]
        in_buf, out_bufs, (in_sem, out_sem) = refs[0], refs[1 : 1 + len(shapes)], refs[1 + len(shapes) :]

        def tile_rows(at):
            return pl.ds(pl.multiple_of(at * tile, tile), tile)

        def in_copies(at):
            return [
                pltpu.make_async_copy(x.at[tile_rows(at)], in_buf.at[i, tile_rows(at)], in_sem.at[i, at])
                for i, x in enumerate(ins)
            ]

        def out_copies(at):
            return [
                pltpu.make_async_copy(
                    out_bufs[i].at[:, :, tile_rows(at)], outs[i].at[:, :, tile_rows(at)], out_sem.at[i, at]
                )
                for i in range(whole)
            ]

        def edge_copy(i):
            return pltpu.make_async_copy(out_bufs[i], outs[i], out_sem.at[i, 0])

        def gather(from_ref, first, count, which, out, at, to):
            def copy(head, carry):
                columns = pl.ds(pl.multiple_of(from_ref[first + head] * HEAD_DIM, HEAD_DIM), HEAD_DIM)
                for index, source in enumerate(which):
                    out[head, index, to, :] = in_buf[source, tile_rows(at), columns]
                return carry

            lax.fori_loop(0, count, copy, 0, unroll=2)

        def each(at, carry):
            for copy in in_copies(at):
                copy.wait()
            for (first, count, which), out in zip(groups, out_bufs):
                gather(scalar_refs[0], first, count, which, out, at, tile_rows(at))
            for copy in out_copies(at):
                copy.start()
            for j, (first, count) in enumerate(edge_groups):
                for i, end in enumerate((0, tiles - 1)):

                    @pl.when(at == end)
                    def _():
                        place = whole + 2 * j + i
                        gather(scalar_refs[1], first, count, range(kinds), out_bufs[place], at, pl.ds(0, tile))
                        edge_copy(place).start()

            return carry

        for at in range(tiles):
            for copy in in_copies(at):
                copy.start()
        lax.fori_loop(0, tiles, each, 0)
        for at in range(tiles):
            for copy in out_copies(at):
                copy.wait()
        for i in range(whole, len(shapes)):
            edge_copy(i).wait()

    smem, anywhere = pl.BlockSpec(memory_space=pltpu.SMEM), pl.BlockSpec(memory_space=pl.ANY)
    dtype = sources[0].dtype
    return pl.pallas_call(
        kernel,
        out_shape=[jax.ShapeDtypeStruct(shape, dtype) for shape in shapes],
        in_specs=[smem] * len(scalars) + [anywhere] * kinds,
        out_specs=[anywhere] * len(shapes),
        scratch_shapes=[pltpu.VMEM((kinds, tokens, width), dtype)]
        + [pltpu.VMEM(shape, dtype) for shape in shapes]
        + [pltpu.SemaphoreType.DMA((kinds, tiles)), pltpu.SemaphoreType.DMA((len(shapes), tiles))],
        compiler_params=pltpu.CompilerParams(vmem_limit_bytes=VMEM_BYTES),
    )(*scalars, *sources)


def attend(query, keys, values, col_mask, biases, flip):
    scores = lax.dot_general(
        keys, query, (((1,), (1,)), ((), ())), preferred_element_type=jnp.float32
    )
    mask = jnp.concatenate([col_mask if x is None else col_mask + x for x in biases], axis=0)
    scores = scores * SCALE + mask
    expo = jnp.exp2(scores - jnp.max(scores, axis=0, keepdims=True))
    probs = (expo * (1.0 / jnp.sum(expo, axis=0, keepdims=True))).astype(jnp.bfloat16)
    left, right = (values, probs) if flip else (probs, values)
    out = lax.dot_general(left, right, (((0,), (0,)), ((), ())), preferred_element_type=jnp.float32)
    return (out.T if flip else out).astype(jnp.bfloat16)


def chunk(meta, flags, col_masks, first, own, given, weights, total_in, last, tile, tiles, unroll=2):
    tokens = tile * tiles
    count = own["query"].shape[0] if own else 0
    sides, corners = (own.get("sides", ()), own.get("corners", ())) if own else ((), ())
    edges = own["edges"] if own else ()
    places = [(start + i, g, i) for g, (start, x) in enumerate(given) for i in range(x.shape[0])]
    places += [(first + i, None, i) for i in range(count)]
    depth = len(places)
    width = weights[0].shape[1] if weights else 0
    blocks, parts = 4, 2
    block, part_width = width // blocks, width // parts
    across = 1 + len(sides)

    def kernel(meta_ref, flag_ref, mask_ref, *refs):
        refs = list(refs)

        def take(items):
            return [refs.pop(0) for _ in items]

        query_ref, pair_ref = take(range(2)) if own else (None, None)
        side_refs, corner_refs = take(sides), take(corners)
        edge_refs = take(edges)
        given_refs, weight_refs = take(given), take(weights)
        total_ref = refs.pop(0) if total_in is not None else None
        out_ref = refs.pop(0)
        if own:
            query_buf, pair_buf, edge_buf, key_buf, value_buf, attended, own_sem, edge_sem = take(range(8))
        side_buf, corner_buf = take(sides[:1]), take(corners[:1])
        given_bufs = take(given)
        if given:
            given_sem = refs.pop(0)
        if weights:
            weight_buf, weight_sem, out_buf, out_sem = take(range(4))
        if total_ref is not None:
            total_buf, total_sem = take(range(2))

        def own_copies(at):
            pairs = [(query_ref.at[at], query_buf.at[at]), (pair_ref.at[at], pair_buf.at[at])]
            pairs += [(x.at[at], side_buf[0].at[at, i]) for i, x in enumerate(side_refs)]
            pairs += [(x.at[at], corner_buf[0].at[at, i]) for i, x in enumerate(corner_refs)]
            return [pltpu.make_async_copy(x, y, own_sem.at[at, i]) for i, (x, y) in enumerate(pairs)]

        def edge_copies(at, slot):
            return [
                pltpu.make_async_copy(x.at[slot], edge_buf.at[at, i], edge_sem.at[at, i])
                for i, x in enumerate(edge_refs)
            ]

        def begin_own(at, carry):
            for copy in own_copies(at):
                copy.start()
            slot = meta_ref[4, first + at]

            if edges:
                for copy in edge_copies(at, jnp.minimum(slot, edges[0].shape[0] - 1)):
                    copy.start()

            return carry

        def given_copy(g):
            return pltpu.make_async_copy(given_refs[g], given_bufs[g], given_sem.at[g])

        def columns(at):
            return pl.ds(pl.multiple_of(at * block, block), block)

        def weight_copy(index, part, source):
            row = pl.multiple_of(meta_ref[6, places[index][0]] * HEAD_DIM, HEAD_DIM)
            wide = pl.ds(pl.multiple_of(part * part_width, part_width), part_width)
            return pltpu.make_async_copy(
                source.at[pl.ds(row, HEAD_DIM), wide],
                weight_buf.at[pl.ds(index * HEAD_DIM, HEAD_DIM), wide],
                weight_sem.at[index, part],
            )

        def total_copy(at):
            return pltpu.make_async_copy(total_ref.at[:, columns(at)], total_buf.at[:, columns(at)], total_sem.at[at])

        def out_copy(at):
            return pltpu.make_async_copy(out_buf.at[:, columns(at)], out_ref.at[:, columns(at)], out_sem.at[at])

        def begin_share(part, carry):
            for index in range(depth):
                mine = meta_ref[5, places[index][0]] == flag_ref[4]

                @pl.when(mine)
                def _():
                    weight_copy(index, part, weight_refs[0]).start()

                @pl.when(jnp.logical_not(mine))
                def _():
                    weight_copy(index, part, weight_refs[1]).start()

            if total_ref is not None:
                for at in range(blocks // parts):
                    total_copy(part * (blocks // parts) + at).start()
            return carry

        def tile_rows(at, size=1):
            return pl.ds(pl.multiple_of(at * tile, tile), size * tile)

        def off(ok):
            return jnp.where(ok, 0.0, NEG_FILL)

        def lay(row, source_k, source_v):
            key_buf[tile_rows(row), :] = source_k
            value_buf[tile_rows(row), :] = source_v

        def head_step(head, carry):
            place = first + head
            rad_f, rad_r, rad_c = meta_ref[1, place], meta_ref[2, place], meta_ref[3, place]
            for copy in own_copies(head) + edge_copies(head, 0):
                copy.wait()
            col_mask = mask_ref[rad_c]
            side_bias = [None] + [off((rad_f > 0) & (flag_ref[i] != 0)) for i in range(across - 1)]
            bodies = [pair_buf.at[head]] + [side_buf[0].at[head, i] for i in range(across - 1)]

            def band_bias(at):
                low = off((rad_r > 0) & ((at > 0) | (flag_ref[2] != 0)))
                high = off((rad_r > 0) & ((at < tiles - 1) | (flag_ref[3] != 0)))
                return low, None, high

            def run(at, start, biases, flip):
                rows, held = tile_rows(at), tile_rows(start, len(biases))
                attended[head, rows, :] = attend(
                    query_buf[head, 0, rows, :], key_buf[held, :], value_buf[held, :], col_mask, biases, flip
                )

            def fill(band):
                def step(at, carry):
                    rows = tile_rows(at)
                    for which, body in enumerate(bodies):
                        lay(across * (at + band) + which, body[0, rows, :], body[1, rows, :])
                    return carry

                lax.fori_loop(0, tiles, step, 0, unroll=2)

            def with_rows():
                ends = [(edge_buf.at[head, 2 * i], edge_buf.at[head, 2 * i + 1]) for i in range(len(edges) // 2)]
                if corners:
                    ends.append((corner_buf[0].at[head, 0], corner_buf[0].at[head, 1]))
                for which, (low, high) in enumerate(ends):
                    lay(which, low[0], low[1])
                    lay(across * (tiles + 1) + which, high[0], high[1])
                fill(1)

                def each(at, carry):
                    biases = []
                    for x in band_bias(at):
                        for y in side_bias:
                            biases.append(x if y is None else y if x is None else jnp.minimum(x, y))
                    run(at, across * at, biases, across > 1)
                    return carry

                lax.fori_loop(0, tiles, each, 0, unroll=tiles if across == 1 else unroll)

            if sides:
                if edges:
                    pl.when(rad_r > 0)(with_rows)

                @pl.when((rad_r == 0) if edges else True)
                def _():
                    fill(0)

                    def each(at, carry):
                        run(at, across * at, side_bias, False)
                        return carry

                    lax.fori_loop(0, tiles, each, 0, unroll=tiles)

            else:
                with_rows()
            return carry

        def share(part, carry):
            for index in range(depth):
                weight_copy(index, part, weight_refs[0]).wait()

            def each(i, carry):
                at = part * (blocks // parts) + i
                held = [attended[i] if g is None else given_bufs[g][i] for _, g, i in places]
                left = jnp.concatenate(held, axis=1)
                total = jnp.dot(left, weight_buf[:, columns(at)], preferred_element_type=jnp.float32)
                if total_ref is not None:
                    total_copy(at).wait()
                    total += total_buf[:, columns(at)]
                out_buf[:, columns(at)] = total.astype(out_buf.dtype)
                out_copy(at).start()
                return carry

            return lax.fori_loop(0, blocks // parts, each, carry)

        def end_share(at, carry):
            out_copy(at).wait()
            return carry

        if own:
            lax.fori_loop(0, count, begin_own, 0)
        for g in range(len(given)):
            given_copy(g).start()
        if weights:
            lax.fori_loop(0, parts, begin_share, 0)
        if own:
            lax.fori_loop(0, count, head_step, 0)
        for g in range(len(given)):
            given_copy(g).wait()
        if weights:
            lax.fori_loop(0, parts, share, 0)
            lax.fori_loop(0, blocks, end_share, 0)
        else:
            done = pltpu.make_async_copy(attended, out_ref, own_sem.at[0, 0])
            done.start()
            done.wait()

    anywhere, smem = pl.BlockSpec(memory_space=pl.ANY), pl.BlockSpec(memory_space=pltpu.SMEM)
    operands, scratch = [], []
    bf16 = jnp.bfloat16
    if own:
        operands += [own["query"], own["pair"], *sides, *corners, *edges]
        kinds = 2 + len(sides) + len(corners)
        scratch += [
            pltpu.VMEM(own["query"].shape, bf16),
            pltpu.VMEM(own["pair"].shape, bf16),
            pltpu.VMEM((count, max(len(edges), 1), 2, tile, HEAD_DIM), bf16),
            pltpu.VMEM((across * (tiles + 2) * tile, HEAD_DIM), bf16),
            pltpu.VMEM((across * (tiles + 2) * tile, HEAD_DIM), bf16),
            pltpu.VMEM((count, tokens, HEAD_DIM), bf16),
            pltpu.SemaphoreType.DMA((count, kinds)),
            pltpu.SemaphoreType.DMA((count, max(len(edges), 1))),
        ]
    if sides:
        scratch.append(pltpu.VMEM((count, 2, 2, tokens, HEAD_DIM), bf16))
    if corners:
        scratch.append(pltpu.VMEM((count, 2, 2, tile, HEAD_DIM), bf16))
    operands += [x for _, x in given]
    scratch += [pltpu.VMEM(x.shape, bf16) for _, x in given]
    if given:
        scratch.append(pltpu.SemaphoreType.DMA((len(given),)))
    out_type = bf16 if last or not weights else jnp.float32
    if weights:
        operands += list(weights)
        scratch += [
            pltpu.VMEM((depth * HEAD_DIM, width), bf16),
            pltpu.SemaphoreType.DMA((depth, parts)),
            pltpu.VMEM((tokens, width), out_type),
            pltpu.SemaphoreType.DMA((blocks,)),
        ]
    if total_in is not None:
        operands.append(total_in)
        scratch += [pltpu.VMEM((tokens, width), jnp.float32), pltpu.SemaphoreType.DMA((blocks,))]
    shape = (tokens, width) if weights else (count, tokens, HEAD_DIM)
    return pl.pallas_call(
        kernel,
        out_shape=jax.ShapeDtypeStruct(shape, out_type),
        in_specs=[smem, smem, pl.BlockSpec(memory_space=pltpu.VMEM)] + [anywhere] * len(operands),
        out_specs=anywhere,
        scratch_shapes=scratch,
        compiler_params=pltpu.CompilerParams(vmem_limit_bytes=VMEM_BYTES),
    )(meta, flags, col_masks, *operands)


def on_device(queries, keys, values, out_weight, window_radii, frame_valid):
    _, rows_dev, col_total, width = queries.shape
    heads = width // HEAD_DIM
    tile = ROW_TILE * col_total
    tiles = rows_dev // ROW_TILE
    tokens = tile * tiles
    frame_pairs, height_total = lax.axis_size("frame"), lax.axis_size("height")
    q, k, v = (x.reshape(tokens, width) for x in (queries, keys, values))
    outer_pairs = [(2 * i + 1, 2 * i + 2) for i in range(frame_pairs - 1)]
    outer_pairs += [(target, source) for source, target in outer_pairs]
    swap = [(0, 1), (1, 0)]
    down = [(i, i + 1) for i in range(height_total - 1)]
    up = [(i + 1, i) for i in range(height_total - 1)]
    levels = [(heads, heads, heads), (16, 10, 16), (13, 8, 14), (10, 6, 12)]

    meta, slots, flags, level = plan_heads(window_radii.T, frame_valid, levels)
    order = meta[0]

    col = np.arange(tile) % col_total // COL_TILE
    gap = np.abs(col[:, None] - col[None, :])
    col_masks = jnp.asarray(np.stack([np.where(gap <= x, 0.0, NEG_FILL) for x in range(2)]).astype(np.float32))

    def trade_edges(low, high):
        return lax.ppermute(high, "height", down), lax.ppermute(low, "height", up)

    def to_sibling(pair):
        return tuple(lax.ppermute(x, "head", swap) for x in pair)

    def trade_corners(beyond):
        return (
            lax.ppermute(beyond[:, :, tokens - tile :], "height", down),
            lax.ppermute(beyond[:, :, :tile], "height", up),
        )

    def finish(side_count, both_count, edge_count):
        def call(q, k, v, out_weight):
            size = both_count if both_count < side_count else side_count // 2
            parts = [(0, size), (size, side_count - size)]
            rest = heads - side_count
            *packed, low, high = pack_heads(
                order, (k, v), [(*x, (0, 1)) for x in parts], tile, tiles, slots, [(0, edge_count)]
            )
            beyond = [lax.ppermute(x, GRID_AXES, outer_pairs) for x in packed]
            beside = [lax.ppermute(x, "head", swap) for x in packed]
            weights = (out_weight, lax.ppermute(out_weight, "head", swap))
            edges = trade_edges(low, high)
            groups = [(*x, (0,)) for x in parts]
            groups += [(side_count, rest, (0,)), (side_count, rest, (1, 2))] if rest else []
            ordered = pack_heads(order, (q, k, v), groups, tile, tiles)
            edges, ordered = lax.optimization_barrier((edges, ordered))
            edges += to_sibling(edges)
            edges, ordered = lax.optimization_barrier((edges, ordered))
            common = (meta, flags, col_masks)
            shared = []
            near = beyond[0]
            if rest:
                own = {"query": ordered[2], "pair": ordered[3], "edges": edges[:2]}
                lone = chunk(*common, side_count, own, [], (), None, False, tile, tiles)
                near, lone = lax.optimization_barrier((near, lone))
            corners = trade_corners(near)
            total = None
            if rest:
                total = chunk(*common, 0, None, [(side_count, lone)], weights, None, False, tile, tiles)
                corners, total = lax.optimization_barrier((corners, total))
            own = {"query": ordered[0], "pair": packed[0], "sides": (beside[0], near), "edges": edges, "corners": corners}
            first = chunk(*common, 0, own, [], (), None, False, tile, tiles, 4)
            far, first = lax.optimization_barrier((beyond[1], first))
            shared.append((0, first))
            own = {"query": ordered[1], "pair": packed[1], "sides": (beside[1], far), "edges": ()}
            if both_count > size:
                own.update({"edges": edges, "corners": trade_corners(far)})
            return chunk(*common, size, own, shared, weights, total, True, tile, tiles)

        return call

    projected = lax.switch(level[0], [finish(*x) for x in levels], q, k, v, out_weight)
    return projected.reshape(1, rows_dev, col_total, out_weight.shape[1])


def solution(mesh):
    return jax.shard_map(
        on_device,
        mesh=mesh,
        in_specs=(
            P(("frame", "head"), "height", None, None),
            P(("frame", "head"), "height", None, None),
            P(("frame", "head"), "height", None, None),
            P("head", None),
            P(),
            P(),
        ),
        out_specs=P(("frame", "head"), "height", None, None),
        check_vma=False,
    )
```

```python
import functools
import math

import jax
import jax.numpy as jnp
import numpy as np
from jax import lax
from jax.experimental import pallas as pl
from jax.experimental.pallas import tpu as pltpu
from jax.sharding import PartitionSpec as P

HEAD_DIM = 128
ROW_TILE = 2
COL_TILE = 16
NEG_FILL = -1e30
GRID_AXES = ("frame", "head")
VMEM_BYTES = 62 * 1024 * 1024
SCALE = HEAD_DIM ** -0.5 * math.log2(math.e)


def plan_heads(window_radii, frame_valid, levels):
    heads = window_radii.shape[1]
    frames = frame_valid.shape[0]

    def kernel(radii_ref, valid_ref, meta_ref, slot_ref, flag_ref, level_ref):
        both, side, edge = (jnp.int32(0) for _ in range(3))
        for head in range(heads):
            rad_f, rad_r = radii_ref[0, head], radii_ref[1, head]
            both += rad_f * rad_r
            side += rad_f * (1 - rad_r)
            edge += (1 - rad_f) * rad_r
        starts = [both + side, heads - edge, both, 0]
        for head in range(heads):
            rad_f, rad_r = radii_ref[0, head], radii_ref[1, head]
            kind = 2 * rad_f + rad_r
            place = sum(jnp.where(kind == i, starts[i], 0) for i in range(4))
            slot = place + jnp.where(kind == 1, both - (heads - edge), jnp.where(kind == 3, 0, edge))
            starts = [starts[i] + (kind == i).astype(jnp.int32) for i in range(4)]
            meta_ref[0, place] = head
            meta_ref[1, place] = rad_f
            meta_ref[2, place] = rad_r
            meta_ref[3, place] = radii_ref[2, head]
            meta_ref[4, place] = slot
            meta_ref[5, place] = head // (heads // 2)
            meta_ref[6, place] = head % (heads // 2)
            slot_ref[slot] = head
        part = lax.axis_index("head")
        frame = 2 * lax.axis_index("frame") + part
        height = lax.axis_index("height")
        inner, outer = frame + 1 - 2 * part, frame - 1 + 2 * part
        outer_ok = (outer >= 0) & (outer < frames) & (valid_ref[jnp.clip(outer, 0, frames - 1)] == 1)
        flag_ref[0] = (valid_ref[inner] == 1).astype(jnp.int32)
        flag_ref[1] = outer_ok.astype(jnp.int32)
        flag_ref[2] = (height > 0).astype(jnp.int32)
        flag_ref[3] = (height < lax.axis_size("height") - 1).astype(jnp.int32)
        flag_ref[4] = part
        level = jnp.int32(0)
        for i, (most_side, most_both, most_edge) in enumerate(levels):
            fits = (both + side <= most_side) & (both <= most_both) & (both + edge <= most_edge)
            fits = fits & ((edge <= heads - most_side) | (most_side == heads))
            level = jnp.where(fits, i, level)
        level_ref[0] = level

    smem = pl.BlockSpec(memory_space=pltpu.SMEM)
    shapes = [(8, heads), (heads,), (8,), (1,)]
    return pl.pallas_call(
        kernel,
        out_shape=[jax.ShapeDtypeStruct(shape, jnp.int32) for shape in shapes],
        in_specs=[smem, smem],
        out_specs=[smem] * len(shapes),
    )(window_radii, frame_valid)


def pack_heads(order, sources, groups, tile, tiles, slots=None, edge_groups=()):
    tokens, width = sources[0].shape
    kinds = len(sources)
    scalars = [order] if slots is None else [order, slots]
    shapes = [(count, len(which), tokens, HEAD_DIM) for _, count, which in groups]
    whole = len(shapes)
    shapes += [(count, kinds, tile, HEAD_DIM) for _, count in edge_groups for _ in range(2)]

    def kernel(*refs):
        scalar_refs, refs = refs[: len(scalars)], refs[len(scalars) :]
        ins, refs = refs[:kinds], refs[kinds:]
        outs, refs = refs[: len(shapes)], refs[len(shapes) :]
        in_buf, out_bufs, (in_sem, out_sem) = refs[0], refs[1 : 1 + len(shapes)], refs[1 + len(shapes) :]

        def tile_rows(at):
            return pl.ds(pl.multiple_of(at * tile, tile), tile)

        def in_copies(at):
            return [
                pltpu.make_async_copy(x.at[tile_rows(at)], in_buf.at[i, tile_rows(at)], in_sem.at[i, at])
                for i, x in enumerate(ins)
            ]

        def out_copies(at):
            return [
                pltpu.make_async_copy(
                    out_bufs[i].at[:, :, tile_rows(at)], outs[i].at[:, :, tile_rows(at)], out_sem.at[i, at]
                )
                for i in range(whole)
            ]

        def edge_copy(i):
            return pltpu.make_async_copy(out_bufs[i], outs[i], out_sem.at[i, 0])

        def gather(from_ref, first, count, which, out, at, to):
            def copy(head, carry):
                columns = pl.ds(pl.multiple_of(from_ref[first + head] * HEAD_DIM, HEAD_DIM), HEAD_DIM)
                for index, source in enumerate(which):
                    out[head, index, to, :] = in_buf[source, tile_rows(at), columns]
                return carry

            lax.fori_loop(0, count, copy, 0, unroll=2)

        def each(at, carry):
            for copy in in_copies(at):
                copy.wait()
            for (first, count, which), out in zip(groups, out_bufs):
                gather(scalar_refs[0], first, count, which, out, at, tile_rows(at))
            for copy in out_copies(at):
                copy.start()
            for j, (first, count) in enumerate(edge_groups):
                for i, end in enumerate((0, tiles - 1)):

                    @pl.when(at == end)
                    def _():
                        place = whole + 2 * j + i
                        gather(scalar_refs[1], first, count, range(kinds), out_bufs[place], at, pl.ds(0, tile))
                        edge_copy(place).start()

            return carry

        for at in range(tiles):
            for copy in in_copies(at):
                copy.start()
        lax.fori_loop(0, tiles, each, 0)
        for at in range(tiles):
            for copy in out_copies(at):
                copy.wait()
        for i in range(whole, len(shapes)):
            edge_copy(i).wait()

    smem, anywhere = pl.BlockSpec(memory_space=pltpu.SMEM), pl.BlockSpec(memory_space=pl.ANY)
    dtype = sources[0].dtype
    return pl.pallas_call(
        kernel,
        out_shape=[jax.ShapeDtypeStruct(shape, dtype) for shape in shapes],
        in_specs=[smem] * len(scalars) + [anywhere] * kinds,
        out_specs=[anywhere] * len(shapes),
        scratch_shapes=[pltpu.VMEM((kinds, tokens, width), dtype)]
        + [pltpu.VMEM(shape, dtype) for shape in shapes]
        + [pltpu.SemaphoreType.DMA((kinds, tiles)), pltpu.SemaphoreType.DMA((len(shapes), tiles))],
        compiler_params=pltpu.CompilerParams(vmem_limit_bytes=VMEM_BYTES),
    )(*scalars, *sources)


def attend(query, keys, values, col_mask, biases, flip):
    scores = lax.dot_general(
        keys, query, (((1,), (1,)), ((), ())), preferred_element_type=jnp.float32
    )
    mask = jnp.concatenate([col_mask if x is None else col_mask + x for x in biases], axis=0)
    scores = scores * SCALE + mask
    expo = jnp.exp2(scores - jnp.max(scores, axis=0, keepdims=True))
    probs = (expo * (1.0 / jnp.sum(expo, axis=0, keepdims=True))).astype(jnp.bfloat16)
    left, right = (values, probs) if flip else (probs, values)
    out = lax.dot_general(left, right, (((0,), (0,)), ((), ())), preferred_element_type=jnp.float32)
    return (out.T if flip else out).astype(jnp.bfloat16)


def chunk(meta, flags, col_masks, first, own, given, weights, total_in, last, tile, tiles, unroll=2):
    tokens = tile * tiles
    count = own["query"].shape[0] if own else 0
    sides, corners = (own.get("sides", ()), own.get("corners", ())) if own else ((), ())
    edges = own["edges"] if own else ()
    places = [(start + i, g, i) for g, (start, x) in enumerate(given) for i in range(x.shape[0])]
    places += [(first + i, None, i) for i in range(count)]
    depth = len(places)
    width = weights[0].shape[1] if weights else 0
    blocks, parts = 4, 2
    block, part_width = width // blocks, width // parts
    across = 1 + len(sides)

    def kernel(meta_ref, flag_ref, mask_ref, *refs):
        refs = list(refs)

        def take(items):
            return [refs.pop(0) for _ in items]

        query_ref, pair_ref = take(range(2)) if own else (None, None)
        side_refs, corner_refs = take(sides), take(corners)
        edge_refs = take(edges)
        given_refs, weight_refs = take(given), take(weights)
        total_ref = refs.pop(0) if total_in is not None else None
        out_ref = refs.pop(0)
        if own:
            query_buf, pair_buf, edge_buf, key_buf, value_buf, attended, own_sem, edge_sem = take(range(8))
        side_buf, corner_buf = take(sides[:1]), take(corners[:1])
        given_bufs = take(given)
        if given:
            given_sem = refs.pop(0)
        if weights:
            weight_buf, weight_sem, out_buf, out_sem = take(range(4))
        if total_ref is not None:
            total_buf, total_sem = take(range(2))

        def own_copies(at):
            pairs = [(query_ref.at[at], query_buf.at[at]), (pair_ref.at[at], pair_buf.at[at])]
            pairs += [(x.at[at], side_buf[0].at[at, i]) for i, x in enumerate(side_refs)]
            pairs += [(x.at[at], corner_buf[0].at[at, i]) for i, x in enumerate(corner_refs)]
            return [pltpu.make_async_copy(x, y, own_sem.at[at, i]) for i, (x, y) in enumerate(pairs)]

        def edge_copies(at, slot):
            return [
                pltpu.make_async_copy(x.at[slot], edge_buf.at[at, i], edge_sem.at[at, i])
                for i, x in enumerate(edge_refs)
            ]

        def begin_own(at, carry):
            for copy in own_copies(at):
                copy.start()
            slot = meta_ref[4, first + at]

            if edges:
                for copy in edge_copies(at, jnp.minimum(slot, edges[0].shape[0] - 1)):
                    copy.start()

            return carry

        def given_copy(g):
            return pltpu.make_async_copy(given_refs[g], given_bufs[g], given_sem.at[g])

        def columns(at):
            return pl.ds(pl.multiple_of(at * block, block), block)

        def weight_copy(index, part, source):
            row = pl.multiple_of(meta_ref[6, places[index][0]] * HEAD_DIM, HEAD_DIM)
            wide = pl.ds(pl.multiple_of(part * part_width, part_width), part_width)
            return pltpu.make_async_copy(
                source.at[pl.ds(row, HEAD_DIM), wide],
                weight_buf.at[pl.ds(index * HEAD_DIM, HEAD_DIM), wide],
                weight_sem.at[index, part],
            )

        def total_copy(at):
            return pltpu.make_async_copy(total_ref.at[:, columns(at)], total_buf.at[:, columns(at)], total_sem.at[at])

        def out_copy(at):
            return pltpu.make_async_copy(out_buf.at[:, columns(at)], out_ref.at[:, columns(at)], out_sem.at[at])

        def begin_share(part, carry):
            for index in range(depth):
                mine = meta_ref[5, places[index][0]] == flag_ref[4]

                @pl.when(mine)
                def _():
                    weight_copy(index, part, weight_refs[0]).start()

                @pl.when(jnp.logical_not(mine))
                def _():
                    weight_copy(index, part, weight_refs[1]).start()

            if total_ref is not None:
                for at in range(blocks // parts):
                    total_copy(part * (blocks // parts) + at).start()
            return carry

        def tile_rows(at, size=1):
            return pl.ds(pl.multiple_of(at * tile, tile), size * tile)

        def off(ok):
            return jnp.where(ok, 0.0, NEG_FILL)

        def lay(row, source_k, source_v):
            key_buf[tile_rows(row), :] = source_k
            value_buf[tile_rows(row), :] = source_v

        def head_step(head, carry):
            place = first + head
            rad_f, rad_r, rad_c = meta_ref[1, place], meta_ref[2, place], meta_ref[3, place]
            for copy in own_copies(head) + edge_copies(head, 0):
                copy.wait()
            col_mask = mask_ref[rad_c]
            side_bias = [None] + [off((rad_f > 0) & (flag_ref[i] != 0)) for i in range(across - 1)]
            bodies = [pair_buf.at[head]] + [side_buf[0].at[head, i] for i in range(across - 1)]

            def band_bias(at):
                low = off((rad_r > 0) & ((at > 0) | (flag_ref[2] != 0)))
                high = off((rad_r > 0) & ((at < tiles - 1) | (flag_ref[3] != 0)))
                return low, None, high

            def run(at, start, biases, flip):
                rows, held = tile_rows(at), tile_rows(start, len(biases))
                attended[head, rows, :] = attend(
                    query_buf[head, 0, rows, :], key_buf[held, :], value_buf[held, :], col_mask, biases, flip
                )

            def fill(band):
                def step(at, carry):
                    rows = tile_rows(at)
                    for which, body in enumerate(bodies):
                        lay(across * (at + band) + which, body[0, rows, :], body[1, rows, :])
                    return carry

                lax.fori_loop(0, tiles, step, 0, unroll=2)

            def with_rows():
                ends = [(edge_buf.at[head, 2 * i], edge_buf.at[head, 2 * i + 1]) for i in range(len(edges) // 2)]
                if corners:
                    ends.append((corner_buf[0].at[head, 0], corner_buf[0].at[head, 1]))
                for which, (low, high) in enumerate(ends):
                    lay(which, low[0], low[1])
                    lay(across * (tiles + 1) + which, high[0], high[1])
                fill(1)

                def each(at, carry):
                    biases = []
                    for x in band_bias(at):
                        for y in side_bias:
                            biases.append(x if y is None else y if x is None else jnp.minimum(x, y))
                    run(at, across * at, biases, across > 1)
                    return carry

                lax.fori_loop(0, tiles, each, 0, unroll=tiles if across == 1 else unroll)

            if sides:
                if edges:
                    pl.when(rad_r > 0)(with_rows)

                @pl.when((rad_r == 0) if edges else True)
                def _():
                    fill(0)

                    def each(at, carry):
                        run(at, across * at, side_bias, False)
                        return carry

                    lax.fori_loop(0, tiles, each, 0, unroll=tiles)

            else:
                with_rows()
            return carry

        def share(part, carry):
            for index in range(depth):
                weight_copy(index, part, weight_refs[0]).wait()

            def each(i, carry):
                at = part * (blocks // parts) + i
                held = [attended[i] if g is None else given_bufs[g][i] for _, g, i in places]
                left = jnp.concatenate(held, axis=1)
                total = jnp.dot(left, weight_buf[:, columns(at)], preferred_element_type=jnp.float32)
                if total_ref is not None:
                    total_copy(at).wait()
                    total += total_buf[:, columns(at)]
                out_buf[:, columns(at)] = total.astype(out_buf.dtype)
                out_copy(at).start()
                return carry

            return lax.fori_loop(0, blocks // parts, each, carry)

        def end_share(at, carry):
            out_copy(at).wait()
            return carry

        if own:
            lax.fori_loop(0, count, begin_own, 0)
        for g in range(len(given)):
            given_copy(g).start()
        if weights:
            lax.fori_loop(0, parts, begin_share, 0)
        if own:
            lax.fori_loop(0, count, head_step, 0)
        for g in range(len(given)):
            given_copy(g).wait()
        if weights:
            lax.fori_loop(0, parts, share, 0)
            lax.fori_loop(0, blocks, end_share, 0)
        else:
            done = pltpu.make_async_copy(attended, out_ref, own_sem.at[0, 0])
            done.start()
            done.wait()

    anywhere, smem = pl.BlockSpec(memory_space=pl.ANY), pl.BlockSpec(memory_space=pltpu.SMEM)
    operands, scratch = [], []
    bf16 = jnp.bfloat16
    if own:
        operands += [own["query"], own["pair"], *sides, *corners, *edges]
        kinds = 2 + len(sides) + len(corners)
        scratch += [
            pltpu.VMEM(own["query"].shape, bf16),
            pltpu.VMEM(own["pair"].shape, bf16),
            pltpu.VMEM((count, max(len(edges), 1), 2, tile, HEAD_DIM), bf16),
            pltpu.VMEM((across * (tiles + 2) * tile, HEAD_DIM), bf16),
            pltpu.VMEM((across * (tiles + 2) * tile, HEAD_DIM), bf16),
            pltpu.VMEM((count, tokens, HEAD_DIM), bf16),
            pltpu.SemaphoreType.DMA((count, kinds)),
            pltpu.SemaphoreType.DMA((count, max(len(edges), 1))),
        ]
    if sides:
        scratch.append(pltpu.VMEM((count, 2, 2, tokens, HEAD_DIM), bf16))
    if corners:
        scratch.append(pltpu.VMEM((count, 2, 2, tile, HEAD_DIM), bf16))
    operands += [x for _, x in given]
    scratch += [pltpu.VMEM(x.shape, bf16) for _, x in given]
    if given:
        scratch.append(pltpu.SemaphoreType.DMA((len(given),)))
    out_type = bf16 if last or not weights else jnp.float32
    if weights:
        operands += list(weights)
        scratch += [
            pltpu.VMEM((depth * HEAD_DIM, width), bf16),
            pltpu.SemaphoreType.DMA((depth, parts)),
            pltpu.VMEM((tokens, width), out_type),
            pltpu.SemaphoreType.DMA((blocks,)),
        ]
    if total_in is not None:
        operands.append(total_in)
        scratch += [pltpu.VMEM((tokens, width), jnp.float32), pltpu.SemaphoreType.DMA((blocks,))]
    shape = (tokens, width) if weights else (count, tokens, HEAD_DIM)
    return pl.pallas_call(
        kernel,
        out_shape=jax.ShapeDtypeStruct(shape, out_type),
        in_specs=[smem, smem, pl.BlockSpec(memory_space=pltpu.VMEM)] + [anywhere] * len(operands),
        out_specs=anywhere,
        scratch_shapes=scratch,
        compiler_params=pltpu.CompilerParams(vmem_limit_bytes=VMEM_BYTES),
    )(meta, flags, col_masks, *operands)


def on_device(queries, keys, values, out_weight, window_radii, frame_valid):
    _, rows_dev, col_total, width = queries.shape
    heads = width // HEAD_DIM
    tile = ROW_TILE * col_total
    tiles = rows_dev // ROW_TILE
    tokens = tile * tiles
    frame_pairs, height_total = lax.axis_size("frame"), lax.axis_size("height")
    q, k, v = (x.reshape(tokens, width) for x in (queries, keys, values))
    outer_pairs = [(2 * i + 1, 2 * i + 2) for i in range(frame_pairs - 1)]
    outer_pairs += [(target, source) for source, target in outer_pairs]
    swap = [(0, 1), (1, 0)]
    down = [(i, i + 1) for i in range(height_total - 1)]
    up = [(i + 1, i) for i in range(height_total - 1)]
    levels = [(heads, heads, heads), (14, 10, 14), (11, 8, 15), (9, 6, 13)]

    meta, slots, flags, level = plan_heads(window_radii.T, frame_valid, levels)
    order = meta[0]

    col = np.arange(tile) % col_total // COL_TILE
    gap = np.abs(col[:, None] - col[None, :])
    col_masks = jnp.asarray(np.stack([np.where(gap <= x, 0.0, NEG_FILL) for x in range(2)]).astype(np.float32))

    def trade_edges(low, high):
        return lax.ppermute(high, "height", down), lax.ppermute(low, "height", up)

    def to_sibling(pair):
        return tuple(lax.ppermute(x, "head", swap) for x in pair)

    def trade_corners(beyond):
        return (
            lax.ppermute(beyond[:, :, tokens - tile :], "height", down),
            lax.ppermute(beyond[:, :, :tile], "height", up),
        )

    def finish(side_count, both_count, edge_count):
        def call(q, k, v, out_weight):
            size = both_count if both_count < side_count else side_count // 2
            parts = [(0, size), (size, side_count - size)]
            rest = heads - side_count
            *packed, low, high = pack_heads(
                order, (k, v), [(*x, (0, 1)) for x in parts], tile, tiles, slots, [(0, edge_count)]
            )
            beyond = [lax.ppermute(x, GRID_AXES, outer_pairs) for x in packed]
            beside = [lax.ppermute(x, "head", swap) for x in packed]
            weights = (out_weight, lax.ppermute(out_weight, "head", swap))
            edges = trade_edges(low, high)
            groups = [(*x, (0,)) for x in parts]
            groups += [(side_count, rest, (0,)), (side_count, rest, (1, 2))] if rest else []
            ordered = pack_heads(order, (q, k, v), groups, tile, tiles)
            edges, ordered = lax.optimization_barrier((edges, ordered))
            edges += to_sibling(edges)
            edges, ordered = lax.optimization_barrier((edges, ordered))
            common = (meta, flags, col_masks)
            shared = []
            near = beyond[0]
            if rest:
                own = {"query": ordered[2], "pair": ordered[3], "edges": edges[:2]}
                lone = chunk(*common, side_count, own, [], (), None, False, tile, tiles)
                near, lone = lax.optimization_barrier((near, lone))
            corners = trade_corners(near)
            total = None
            if rest:
                total = chunk(*common, 0, None, [(side_count, lone)], weights, None, False, tile, tiles)
                corners, total = lax.optimization_barrier((corners, total))
            own = {"query": ordered[0], "pair": packed[0], "sides": (beside[0], near), "edges": edges, "corners": corners}
            first = chunk(*common, 0, own, [], (), None, False, tile, tiles, 4)
            far, first = lax.optimization_barrier((beyond[1], first))
            shared.append((0, first))
            own = {"query": ordered[1], "pair": packed[1], "sides": (beside[1], far), "edges": ()}
            if both_count > size:
                own.update({"edges": edges, "corners": trade_corners(far)})
            return chunk(*common, size, own, shared, weights, total, True, tile, tiles)

        return call

    projected = lax.switch(level[0], [finish(*x) for x in levels], q, k, v, out_weight)
    return projected.reshape(1, rows_dev, col_total, out_weight.shape[1])


def solution(mesh):
    return jax.shard_map(
        on_device,
        mesh=mesh,
        in_specs=(
            P(("frame", "head"), "height", None, None),
            P(("frame", "head"), "height", None, None),
            P(("frame", "head"), "height", None, None),
            P("head", None),
            P(),
            P(),
        ),
        out_specs=P(("frame", "head"), "height", None, None),
        check_vma=False,
    )
```

```python
import functools
import math

import jax
import jax.numpy as jnp
import numpy as np
from jax import lax
from jax.experimental import pallas as pl
from jax.experimental.pallas import tpu as pltpu
from jax.sharding import PartitionSpec as P

HEAD_DIM = 128
ROW_TILE = 2
COL_TILE = 16
NEG_FILL = -1e30
GRID_AXES = ("frame", "head")
VMEM_BYTES = 62 * 1024 * 1024
SCALE = HEAD_DIM ** -0.5 * math.log2(math.e)


def plan_heads(window_radii, frame_valid, levels):
    heads = window_radii.shape[1]
    frames = frame_valid.shape[0]

    def kernel(radii_ref, valid_ref, meta_ref, slot_ref, flag_ref, level_ref):
        both, side, edge = (jnp.int32(0) for _ in range(3))
        for head in range(heads):
            rad_f, rad_r = radii_ref[0, head], radii_ref[1, head]
            both += rad_f * rad_r
            side += rad_f * (1 - rad_r)
            edge += (1 - rad_f) * rad_r
        starts = [both + side, heads - edge, both, 0]
        for head in range(heads):
            rad_f, rad_r = radii_ref[0, head], radii_ref[1, head]
            kind = 2 * rad_f + rad_r
            place = sum(jnp.where(kind == i, starts[i], 0) for i in range(4))
            slot = place + jnp.where(kind == 1, both - (heads - edge), jnp.where(kind == 3, 0, edge))
            starts = [starts[i] + (kind == i).astype(jnp.int32) for i in range(4)]
            meta_ref[0, place] = head
            meta_ref[1, place] = rad_f
            meta_ref[2, place] = rad_r
            meta_ref[3, place] = radii_ref[2, head]
            meta_ref[4, place] = slot
            meta_ref[5, place] = head // (heads // 2)
            meta_ref[6, place] = head % (heads // 2)
            slot_ref[slot] = head
        part = lax.axis_index("head")
        frame = 2 * lax.axis_index("frame") + part
        height = lax.axis_index("height")
        inner, outer = frame + 1 - 2 * part, frame - 1 + 2 * part
        outer_ok = (outer >= 0) & (outer < frames) & (valid_ref[jnp.clip(outer, 0, frames - 1)] == 1)
        flag_ref[0] = (valid_ref[inner] == 1).astype(jnp.int32)
        flag_ref[1] = outer_ok.astype(jnp.int32)
        flag_ref[2] = (height > 0).astype(jnp.int32)
        flag_ref[3] = (height < lax.axis_size("height") - 1).astype(jnp.int32)
        flag_ref[4] = part
        level = jnp.int32(0)
        for i, (most_side, most_both, most_edge) in enumerate(levels):
            fits = (both + side <= most_side) & (both <= most_both) & (both + edge <= most_edge)
            fits = fits & ((edge <= heads - most_side) | (most_side == heads))
            level = jnp.where(fits, i, level)
        level_ref[0] = level

    smem = pl.BlockSpec(memory_space=pltpu.SMEM)
    shapes = [(8, heads), (heads,), (8,), (1,)]
    return pl.pallas_call(
        kernel,
        out_shape=[jax.ShapeDtypeStruct(shape, jnp.int32) for shape in shapes],
        in_specs=[smem, smem],
        out_specs=[smem] * len(shapes),
    )(window_radii, frame_valid)


def pack_heads(order, sources, groups, tile, tiles, slots=None, edge_groups=()):
    tokens, width = sources[0].shape
    kinds = len(sources)
    scalars = [order] if slots is None else [order, slots]
    shapes = [(count, len(which), tokens, HEAD_DIM) for _, count, which in groups]
    whole = len(shapes)
    shapes += [(count, kinds, tile, HEAD_DIM) for _, count in edge_groups for _ in range(2)]

    def kernel(*refs):
        scalar_refs, refs = refs[: len(scalars)], refs[len(scalars) :]
        ins, refs = refs[:kinds], refs[kinds:]
        outs, refs = refs[: len(shapes)], refs[len(shapes) :]
        in_buf, out_bufs, (in_sem, out_sem) = refs[0], refs[1 : 1 + len(shapes)], refs[1 + len(shapes) :]

        def tile_rows(at):
            return pl.ds(pl.multiple_of(at * tile, tile), tile)

        def in_copies(at):
            return [
                pltpu.make_async_copy(x.at[tile_rows(at)], in_buf.at[i, tile_rows(at)], in_sem.at[i, at])
                for i, x in enumerate(ins)
            ]

        def out_copies(at):
            return [
                pltpu.make_async_copy(
                    out_bufs[i].at[:, :, tile_rows(at)], outs[i].at[:, :, tile_rows(at)], out_sem.at[i, at]
                )
                for i in range(whole)
            ]

        def edge_copy(i):
            return pltpu.make_async_copy(out_bufs[i], outs[i], out_sem.at[i, 0])

        def gather(from_ref, first, count, which, out, at, to):
            def copy(head, carry):
                columns = pl.ds(pl.multiple_of(from_ref[first + head] * HEAD_DIM, HEAD_DIM), HEAD_DIM)
                for index, source in enumerate(which):
                    out[head, index, to, :] = in_buf[source, tile_rows(at), columns]
                return carry

            lax.fori_loop(0, count, copy, 0, unroll=2)

        def each(at, carry):
            for copy in in_copies(at):
                copy.wait()
            for (first, count, which), out in zip(groups, out_bufs):
                gather(scalar_refs[0], first, count, which, out, at, tile_rows(at))
            for copy in out_copies(at):
                copy.start()
            for j, (first, count) in enumerate(edge_groups):
                for i, end in enumerate((0, tiles - 1)):

                    @pl.when(at == end)
                    def _():
                        place = whole + 2 * j + i
                        gather(scalar_refs[1], first, count, range(kinds), out_bufs[place], at, pl.ds(0, tile))
                        edge_copy(place).start()

            return carry

        for at in range(tiles):
            for copy in in_copies(at):
                copy.start()
        lax.fori_loop(0, tiles, each, 0)
        for at in range(tiles):
            for copy in out_copies(at):
                copy.wait()
        for i in range(whole, len(shapes)):
            edge_copy(i).wait()

    smem, anywhere = pl.BlockSpec(memory_space=pltpu.SMEM), pl.BlockSpec(memory_space=pl.ANY)
    dtype = sources[0].dtype
    return pl.pallas_call(
        kernel,
        out_shape=[jax.ShapeDtypeStruct(shape, dtype) for shape in shapes],
        in_specs=[smem] * len(scalars) + [anywhere] * kinds,
        out_specs=[anywhere] * len(shapes),
        scratch_shapes=[pltpu.VMEM((kinds, tokens, width), dtype)]
        + [pltpu.VMEM(shape, dtype) for shape in shapes]
        + [pltpu.SemaphoreType.DMA((kinds, tiles)), pltpu.SemaphoreType.DMA((len(shapes), tiles))],
        compiler_params=pltpu.CompilerParams(vmem_limit_bytes=VMEM_BYTES),
    )(*scalars, *sources)


def attend(query, keys, values, col_mask, biases, flip):
    scores = lax.dot_general(
        keys, query, (((1,), (1,)), ((), ())), preferred_element_type=jnp.float32
    )
    mask = jnp.concatenate([col_mask if x is None else col_mask + x for x in biases], axis=0)
    scores = scores * SCALE + mask
    expo = jnp.exp2(scores - jnp.max(scores, axis=0, keepdims=True))
    probs = (expo * (1.0 / jnp.sum(expo, axis=0, keepdims=True))).astype(jnp.bfloat16)
    left, right = (values, probs) if flip else (probs, values)
    out = lax.dot_general(left, right, (((0,), (0,)), ((), ())), preferred_element_type=jnp.float32)
    return (out.T if flip else out).astype(jnp.bfloat16)


def chunk(meta, flags, col_masks, first, own, given, weights, total_in, last, tile, tiles, unroll=2):
    tokens = tile * tiles
    count = own["query"].shape[0] if own else 0
    sides, corners = (own.get("sides", ()), own.get("corners", ())) if own else ((), ())
    edges = own["edges"] if own else ()
    places = [(start + i, g, i) for g, (start, x) in enumerate(given) for i in range(x.shape[0])]
    places += [(first + i, None, i) for i in range(count)]
    depth = len(places)
    width = weights[0].shape[1] if weights else 0
    blocks, parts = 4, 2 if own else 4
    block, part_width = width // blocks, width // parts
    across = 1 + len(sides)

    def kernel(meta_ref, flag_ref, mask_ref, *refs):
        refs = list(refs)

        def take(items):
            return [refs.pop(0) for _ in items]

        query_ref, pair_ref = take(range(2)) if own else (None, None)
        side_refs, corner_refs = take(sides), take(corners)
        edge_refs = take(edges)
        given_refs, weight_refs = take(given), take(weights)
        total_ref = refs.pop(0) if total_in is not None else None
        out_ref = refs.pop(0)
        if own:
            query_buf, pair_buf, edge_buf, key_buf, value_buf, attended, own_sem, edge_sem = take(range(8))
        side_buf, corner_buf = take(sides[:1]), take(corners[:1])
        given_bufs = take(given)
        if given:
            given_sem = refs.pop(0)
        if weights:
            weight_buf, weight_sem, out_buf, out_sem = take(range(4))
        if total_ref is not None:
            total_buf, total_sem = take(range(2))

        def own_copies(at):
            pairs = [(query_ref.at[at], query_buf.at[at]), (pair_ref.at[at], pair_buf.at[at])]
            pairs += [(x.at[at], side_buf[0].at[at, i]) for i, x in enumerate(side_refs)]
            pairs += [(x.at[at], corner_buf[0].at[at, i]) for i, x in enumerate(corner_refs)]
            return [pltpu.make_async_copy(x, y, own_sem.at[at, i]) for i, (x, y) in enumerate(pairs)]

        def edge_copies(at, slot):
            return [
                pltpu.make_async_copy(x.at[slot], edge_buf.at[at, i], edge_sem.at[at, i])
                for i, x in enumerate(edge_refs)
            ]

        def begin_own(at, carry):
            for copy in own_copies(at):
                copy.start()
            slot = meta_ref[4, first + at]

            if edges:
                for copy in edge_copies(at, jnp.minimum(slot, edges[0].shape[0] - 1)):
                    copy.start()

            return carry

        def given_copy(g):
            return pltpu.make_async_copy(given_refs[g], given_bufs[g], given_sem.at[g])

        def columns(at):
            return pl.ds(pl.multiple_of(at * block, block), block)

        def weight_copy(index, part, source):
            row = pl.multiple_of(meta_ref[6, places[index][0]] * HEAD_DIM, HEAD_DIM)
            wide = pl.ds(pl.multiple_of(part * part_width, part_width), part_width)
            return pltpu.make_async_copy(
                source.at[pl.ds(row, HEAD_DIM), wide],
                weight_buf.at[pl.ds(index * HEAD_DIM, HEAD_DIM), wide],
                weight_sem.at[index, part],
            )

        def total_copy(at):
            return pltpu.make_async_copy(total_ref.at[:, columns(at)], total_buf.at[:, columns(at)], total_sem.at[at])

        def out_copy(at):
            return pltpu.make_async_copy(out_buf.at[:, columns(at)], out_ref.at[:, columns(at)], out_sem.at[at])

        def begin_share(part, carry):
            for index in range(depth):
                mine = meta_ref[5, places[index][0]] == flag_ref[4]

                @pl.when(mine)
                def _():
                    weight_copy(index, part, weight_refs[0]).start()

                @pl.when(jnp.logical_not(mine))
                def _():
                    weight_copy(index, part, weight_refs[1]).start()

            if total_ref is not None:
                for at in range(blocks // parts):
                    total_copy(part * (blocks // parts) + at).start()
            return carry

        def tile_rows(at, size=1):
            return pl.ds(pl.multiple_of(at * tile, tile), size * tile)

        def off(ok):
            return jnp.where(ok, 0.0, NEG_FILL)

        def lay(row, source_k, source_v):
            key_buf[tile_rows(row), :] = source_k
            value_buf[tile_rows(row), :] = source_v

        def head_step(head, carry):
            place = first + head
            rad_f, rad_r, rad_c = meta_ref[1, place], meta_ref[2, place], meta_ref[3, place]
            for copy in own_copies(head) + edge_copies(head, 0):
                copy.wait()
            col_mask = mask_ref[rad_c]
            side_bias = [None] + [off((rad_f > 0) & (flag_ref[i] != 0)) for i in range(across - 1)]
            bodies = [pair_buf.at[head]] + [side_buf[0].at[head, i] for i in range(across - 1)]

            def band_bias(at):
                low = off((rad_r > 0) & ((at > 0) | (flag_ref[2] != 0)))
                high = off((rad_r > 0) & ((at < tiles - 1) | (flag_ref[3] != 0)))
                return low, None, high

            def run(at, start, biases, flip):
                rows, held = tile_rows(at), tile_rows(start, len(biases))
                attended[head, rows, :] = attend(
                    query_buf[head, 0, rows, :], key_buf[held, :], value_buf[held, :], col_mask, biases, flip
                )

            def fill(band):
                def step(at, carry):
                    rows = tile_rows(at)
                    for which, body in enumerate(bodies):
                        lay(across * (at + band) + which, body[0, rows, :], body[1, rows, :])
                    return carry

                lax.fori_loop(0, tiles, step, 0, unroll=2)

            def with_rows():
                ends = [(edge_buf.at[head, 2 * i], edge_buf.at[head, 2 * i + 1]) for i in range(len(edges) // 2)]
                if corners:
                    ends.append((corner_buf[0].at[head, 0], corner_buf[0].at[head, 1]))
                for which, (low, high) in enumerate(ends):
                    lay(which, low[0], low[1])
                    lay(across * (tiles + 1) + which, high[0], high[1])
                fill(1)

                def each(at, carry):
                    biases = []
                    for x in band_bias(at):
                        for y in side_bias:
                            biases.append(x if y is None else y if x is None else jnp.minimum(x, y))
                    run(at, across * at, biases, across > 1)
                    return carry

                lax.fori_loop(0, tiles, each, 0, unroll=tiles if across == 1 else unroll)

            if sides:
                if edges:
                    pl.when(rad_r > 0)(with_rows)

                @pl.when((rad_r == 0) if edges else True)
                def _():
                    fill(0)

                    def each(at, carry):
                        run(at, across * at, side_bias, False)
                        return carry

                    lax.fori_loop(0, tiles, each, 0, unroll=tiles)

            else:
                with_rows()
            return carry

        def share(part, carry):
            for index in range(depth):
                weight_copy(index, part, weight_refs[0]).wait()

            def each(i, carry):
                at = part * (blocks // parts) + i
                held = [attended[i] if g is None else given_bufs[g][i] for _, g, i in places]
                left = jnp.concatenate(held, axis=1)
                total = jnp.dot(left, weight_buf[:, columns(at)], preferred_element_type=jnp.float32)
                if total_ref is not None:
                    total_copy(at).wait()
                    total += total_buf[:, columns(at)]
                out_buf[:, columns(at)] = total.astype(out_buf.dtype)
                out_copy(at).start()
                return carry

            return lax.fori_loop(0, blocks // parts, each, carry)

        def end_share(at, carry):
            out_copy(at).wait()
            return carry

        if own:
            lax.fori_loop(0, count, begin_own, 0)
        for g in range(len(given)):
            given_copy(g).start()
        if weights:
            lax.fori_loop(0, parts, begin_share, 0)
        if own:
            lax.fori_loop(0, count, head_step, 0)
        for g in range(len(given)):
            given_copy(g).wait()
        if weights:
            lax.fori_loop(0, parts, share, 0)
            lax.fori_loop(0, blocks, end_share, 0)
        else:
            done = pltpu.make_async_copy(attended, out_ref, own_sem.at[0, 0])
            done.start()
            done.wait()

    anywhere, smem = pl.BlockSpec(memory_space=pl.ANY), pl.BlockSpec(memory_space=pltpu.SMEM)
    operands, scratch = [], []
    bf16 = jnp.bfloat16
    if own:
        operands += [own["query"], own["pair"], *sides, *corners, *edges]
        kinds = 2 + len(sides) + len(corners)
        scratch += [
            pltpu.VMEM(own["query"].shape, bf16),
            pltpu.VMEM(own["pair"].shape, bf16),
            pltpu.VMEM((count, max(len(edges), 1), 2, tile, HEAD_DIM), bf16),
            pltpu.VMEM((across * (tiles + 2) * tile, HEAD_DIM), bf16),
            pltpu.VMEM((across * (tiles + 2) * tile, HEAD_DIM), bf16),
            pltpu.VMEM((count, tokens, HEAD_DIM), bf16),
            pltpu.SemaphoreType.DMA((count, kinds)),
            pltpu.SemaphoreType.DMA((count, max(len(edges), 1))),
        ]
    if sides:
        scratch.append(pltpu.VMEM((count, 2, 2, tokens, HEAD_DIM), bf16))
    if corners:
        scratch.append(pltpu.VMEM((count, 2, 2, tile, HEAD_DIM), bf16))
    operands += [x for _, x in given]
    scratch += [pltpu.VMEM(x.shape, bf16) for _, x in given]
    if given:
        scratch.append(pltpu.SemaphoreType.DMA((len(given),)))
    out_type = bf16 if last or not weights else jnp.float32
    if weights:
        operands += list(weights)
        scratch += [
            pltpu.VMEM((depth * HEAD_DIM, width), bf16),
            pltpu.SemaphoreType.DMA((depth, parts)),
            pltpu.VMEM((tokens, width), out_type),
            pltpu.SemaphoreType.DMA((blocks,)),
        ]
    if total_in is not None:
        operands.append(total_in)
        scratch += [pltpu.VMEM((tokens, width), jnp.float32), pltpu.SemaphoreType.DMA((blocks,))]
    shape = (tokens, width) if weights else (count, tokens, HEAD_DIM)
    return pl.pallas_call(
        kernel,
        out_shape=jax.ShapeDtypeStruct(shape, out_type),
        in_specs=[smem, smem, pl.BlockSpec(memory_space=pltpu.VMEM)] + [anywhere] * len(operands),
        out_specs=anywhere,
        scratch_shapes=scratch,
        compiler_params=pltpu.CompilerParams(vmem_limit_bytes=VMEM_BYTES),
    )(meta, flags, col_masks, *operands)


def on_device(queries, keys, values, out_weight, window_radii, frame_valid):
    _, rows_dev, col_total, width = queries.shape
    heads = width // HEAD_DIM
    tile = ROW_TILE * col_total
    tiles = rows_dev // ROW_TILE
    tokens = tile * tiles
    frame_pairs, height_total = lax.axis_size("frame"), lax.axis_size("height")
    q, k, v = (x.reshape(tokens, width) for x in (queries, keys, values))
    outer_pairs = [(2 * i + 1, 2 * i + 2) for i in range(frame_pairs - 1)]
    outer_pairs += [(target, source) for source, target in outer_pairs]
    swap = [(0, 1), (1, 0)]
    down = [(i, i + 1) for i in range(height_total - 1)]
    up = [(i + 1, i) for i in range(height_total - 1)]
    levels = [(heads, heads, heads), (14, 10, 14), (11, 8, 15), (9, 6, 13)]

    meta, slots, flags, level = plan_heads(window_radii.T, frame_valid, levels)
    order = meta[0]

    col = np.arange(tile) % col_total // COL_TILE
    gap = np.abs(col[:, None] - col[None, :])
    col_masks = jnp.asarray(np.stack([np.where(gap <= x, 0.0, NEG_FILL) for x in range(2)]).astype(np.float32))

    def trade_edges(low, high):
        return lax.ppermute(high, "height", down), lax.ppermute(low, "height", up)

    def to_sibling(pair):
        return tuple(lax.ppermute(x, "head", swap) for x in pair)

    def trade_corners(beyond):
        return (
            lax.ppermute(beyond[:, :, tokens - tile :], "height", down),
            lax.ppermute(beyond[:, :, :tile], "height", up),
        )

    def finish(side_count, both_count, edge_count):
        def call(q, k, v, out_weight):
            size = both_count if both_count < side_count else side_count // 2
            parts = [(0, size), (size, side_count - size)]
            rest = heads - side_count
            *packed, low, high = pack_heads(
                order, (k, v), [(*x, (0, 1)) for x in parts], tile, tiles, slots, [(0, edge_count)]
            )
            beyond = [lax.ppermute(x, GRID_AXES, outer_pairs) for x in packed]
            beside = [lax.ppermute(x, "head", swap) for x in packed]
            weights = (out_weight, lax.ppermute(out_weight, "head", swap))
            edges = trade_edges(low, high)
            groups = [(*x, (0,)) for x in parts]
            groups += [(side_count, rest, (0,)), (side_count, rest, (1, 2))] if rest else []
            ordered = pack_heads(order, (q, k, v), groups, tile, tiles)
            edges, ordered = lax.optimization_barrier((edges, ordered))
            edges += to_sibling(edges)
            edges, ordered = lax.optimization_barrier((edges, ordered))
            common = (meta, flags, col_masks)
            shared = []
            near = beyond[0]
            if rest:
                own = {"query": ordered[2], "pair": ordered[3], "edges": edges[:2]}
                lone = chunk(*common, side_count, own, [], (), None, False, tile, tiles)
                near, lone = lax.optimization_barrier((near, lone))
            corners = trade_corners(near)
            total = None
            if rest:
                total = chunk(*common, 0, None, [(side_count, lone)], weights, None, False, tile, tiles)
                corners, total = lax.optimization_barrier((corners, total))
            own = {"query": ordered[0], "pair": packed[0], "sides": (beside[0], near), "edges": edges, "corners": corners}
            first = chunk(*common, 0, own, [], (), None, False, tile, tiles, 4)
            far, first = lax.optimization_barrier((beyond[1], first))
            shared.append((0, first))
            own = {"query": ordered[1], "pair": packed[1], "sides": (beside[1], far), "edges": ()}
            if both_count > size:
                own.update({"edges": edges, "corners": trade_corners(far)})
            return chunk(*common, size, own, shared, weights, total, True, tile, tiles)

        return call

    projected = lax.switch(level[0], [finish(*x) for x in levels], q, k, v, out_weight)
    return projected.reshape(1, rows_dev, col_total, out_weight.shape[1])


def solution(mesh):
    return jax.shard_map(
        on_device,
        mesh=mesh,
        in_specs=(
            P(("frame", "head"), "height", None, None),
            P(("frame", "head"), "height", None, None),
            P(("frame", "head"), "height", None, None),
            P("head", None),
            P(),
            P(),
        ),
        out_specs=P(("frame", "head"), "height", None, None),
        check_vma=False,
    )
```

```python
import functools
import math

import jax
import jax.numpy as jnp
import numpy as np
from jax import lax
from jax.experimental import pallas as pl
from jax.experimental.pallas import tpu as pltpu
from jax.sharding import PartitionSpec as P

HEAD_DIM = 128
ROW_TILE = 2
COL_TILE = 16
NEG_FILL = -1e30
GRID_AXES = ("frame", "head")
VMEM_BYTES = 62 * 1024 * 1024
SCALE = HEAD_DIM ** -0.5 * math.log2(math.e)


def plan_heads(window_radii, frame_valid, levels):
    heads = window_radii.shape[1]
    frames = frame_valid.shape[0]

    def kernel(radii_ref, valid_ref, meta_ref, slot_ref, flag_ref, level_ref):
        both, side, edge = (jnp.int32(0) for _ in range(3))
        for head in range(heads):
            rad_f, rad_r = radii_ref[0, head], radii_ref[1, head]
            both += rad_f * rad_r
            side += rad_f * (1 - rad_r)
            edge += (1 - rad_f) * rad_r
        starts = [both + side, heads - edge, both, 0]
        for head in range(heads):
            rad_f, rad_r = radii_ref[0, head], radii_ref[1, head]
            kind = 2 * rad_f + rad_r
            place = sum(jnp.where(kind == i, starts[i], 0) for i in range(4))
            slot = place + jnp.where(kind == 1, both - (heads - edge), jnp.where(kind == 3, 0, edge))
            starts = [starts[i] + (kind == i).astype(jnp.int32) for i in range(4)]
            meta_ref[0, place] = head
            meta_ref[1, place] = rad_f
            meta_ref[2, place] = rad_r
            meta_ref[3, place] = radii_ref[2, head]
            meta_ref[4, place] = slot
            meta_ref[5, place] = head // (heads // 2)
            meta_ref[6, place] = head % (heads // 2)
            slot_ref[slot] = head
        part = lax.axis_index("head")
        frame = 2 * lax.axis_index("frame") + part
        height = lax.axis_index("height")
        inner, outer = frame + 1 - 2 * part, frame - 1 + 2 * part
        outer_ok = (outer >= 0) & (outer < frames) & (valid_ref[jnp.clip(outer, 0, frames - 1)] == 1)
        flag_ref[0] = (valid_ref[inner] == 1).astype(jnp.int32)
        flag_ref[1] = outer_ok.astype(jnp.int32)
        flag_ref[2] = (height > 0).astype(jnp.int32)
        flag_ref[3] = (height < lax.axis_size("height") - 1).astype(jnp.int32)
        flag_ref[4] = part
        level = jnp.int32(0)
        for i, (most_side, most_both, most_edge) in enumerate(levels):
            fits = (both + side <= most_side) & (both <= most_both) & (both + edge <= most_edge)
            fits = fits & ((edge <= heads - most_side) | (most_side == heads))
            level = jnp.where(fits, i, level)
        level_ref[0] = level

    smem = pl.BlockSpec(memory_space=pltpu.SMEM)
    shapes = [(8, heads), (heads,), (8,), (1,)]
    return pl.pallas_call(
        kernel,
        out_shape=[jax.ShapeDtypeStruct(shape, jnp.int32) for shape in shapes],
        in_specs=[smem, smem],
        out_specs=[smem] * len(shapes),
    )(window_radii, frame_valid)


def pack_heads(order, sources, groups, tile, tiles, slots=None, edge_groups=()):
    tokens, width = sources[0].shape
    kinds = len(sources)
    scalars = [order] if slots is None else [order, slots]
    shapes = [(count, len(which), tokens, HEAD_DIM) for _, count, which in groups]
    whole = len(shapes)
    shapes += [(count, kinds, tile, HEAD_DIM) for _, count in edge_groups for _ in range(2)]

    def kernel(*refs):
        scalar_refs, refs = refs[: len(scalars)], refs[len(scalars) :]
        ins, refs = refs[:kinds], refs[kinds:]
        outs, refs = refs[: len(shapes)], refs[len(shapes) :]
        in_buf, out_bufs, (in_sem, out_sem) = refs[0], refs[1 : 1 + len(shapes)], refs[1 + len(shapes) :]

        def tile_rows(at):
            return pl.ds(pl.multiple_of(at * tile, tile), tile)

        def in_copies(at):
            return [
                pltpu.make_async_copy(x.at[tile_rows(at)], in_buf.at[i, tile_rows(at)], in_sem.at[i, at])
                for i, x in enumerate(ins)
            ]

        def out_copies(at):
            return [
                pltpu.make_async_copy(
                    out_bufs[i].at[:, :, tile_rows(at)], outs[i].at[:, :, tile_rows(at)], out_sem.at[i, at]
                )
                for i in range(whole)
            ]

        def edge_copy(i):
            return pltpu.make_async_copy(out_bufs[i], outs[i], out_sem.at[i, 0])

        def gather(from_ref, first, count, which, out, at, to):
            def copy(head, carry):
                columns = pl.ds(pl.multiple_of(from_ref[first + head] * HEAD_DIM, HEAD_DIM), HEAD_DIM)
                for index, source in enumerate(which):
                    out[head, index, to, :] = in_buf[source, tile_rows(at), columns]
                return carry

            lax.fori_loop(0, count, copy, 0, unroll=2)

        def each(at, carry):
            for copy in in_copies(at):
                copy.wait()
            for (first, count, which), out in zip(groups, out_bufs):
                gather(scalar_refs[0], first, count, which, out, at, tile_rows(at))
            for copy in out_copies(at):
                copy.start()
            for j, (first, count) in enumerate(edge_groups):
                for i, end in enumerate((0, tiles - 1)):

                    @pl.when(at == end)
                    def _():
                        place = whole + 2 * j + i
                        gather(scalar_refs[1], first, count, range(kinds), out_bufs[place], at, pl.ds(0, tile))
                        edge_copy(place).start()

            return carry

        for at in range(tiles):
            for copy in in_copies(at):
                copy.start()
        lax.fori_loop(0, tiles, each, 0)
        for at in range(tiles):
            for copy in out_copies(at):
                copy.wait()
        for i in range(whole, len(shapes)):
            edge_copy(i).wait()

    smem, anywhere = pl.BlockSpec(memory_space=pltpu.SMEM), pl.BlockSpec(memory_space=pl.ANY)
    dtype = sources[0].dtype
    return pl.pallas_call(
        kernel,
        out_shape=[jax.ShapeDtypeStruct(shape, dtype) for shape in shapes],
        in_specs=[smem] * len(scalars) + [anywhere] * kinds,
        out_specs=[anywhere] * len(shapes),
        scratch_shapes=[pltpu.VMEM((kinds, tokens, width), dtype)]
        + [pltpu.VMEM(shape, dtype) for shape in shapes]
        + [pltpu.SemaphoreType.DMA((kinds, tiles)), pltpu.SemaphoreType.DMA((len(shapes), tiles))],
        compiler_params=pltpu.CompilerParams(vmem_limit_bytes=VMEM_BYTES),
    )(*scalars, *sources)


def attend(query, keys, values, col_mask, biases, flip):
    scores = lax.dot_general(
        keys, query, (((1,), (1,)), ((), ())), preferred_element_type=jnp.float32
    )
    mask = jnp.concatenate([col_mask if x is None else col_mask + x for x in biases], axis=0)
    scores = scores * SCALE + mask
    expo = jnp.exp2(scores - jnp.max(scores, axis=0, keepdims=True))
    probs = (expo * (1.0 / jnp.sum(expo, axis=0, keepdims=True))).astype(jnp.bfloat16)
    left, right = (values, probs) if flip else (probs, values)
    out = lax.dot_general(left, right, (((0,), (0,)), ((), ())), preferred_element_type=jnp.float32)
    return (out.T if flip else out).astype(jnp.bfloat16)


def chunk(meta, flags, col_masks, first, own, given, weights, total_in, last, tile, tiles, unroll=2):
    tokens = tile * tiles
    count = own["query"].shape[0] if own else 0
    sides, corners = (own.get("sides", ()), own.get("corners", ())) if own else ((), ())
    edges = own["edges"] if own else ()
    places = [(start + i, g, i) for g, (start, x) in enumerate(given) for i in range(x.shape[0])]
    places += [(first + i, None, i) for i in range(count)]
    depth = len(places)
    width = weights[0].shape[1] if weights else 0
    blocks, parts = 4, 2 if own else 4
    block, part_width = width // blocks, width // parts
    across = 1 + len(sides)

    def kernel(meta_ref, flag_ref, mask_ref, *refs):
        refs = list(refs)

        def take(items):
            return [refs.pop(0) for _ in items]

        query_ref, pair_ref = take(range(2)) if own else (None, None)
        side_refs, corner_refs = take(sides), take(corners)
        edge_refs = take(edges)
        given_refs, weight_refs = take(given), take(weights)
        total_ref = refs.pop(0) if total_in is not None else None
        out_ref = refs.pop(0)
        if own:
            query_buf, pair_buf, edge_buf, key_buf, value_buf, attended, own_sem, edge_sem = take(range(8))
        side_buf, corner_buf = take(sides[:1]), take(corners[:1])
        given_bufs = take(given)
        if given:
            given_sem = refs.pop(0)
        if weights:
            weight_buf, weight_sem, out_buf, out_sem = take(range(4))
        if total_ref is not None:
            total_buf, total_sem = take(range(2))

        def own_copies(at):
            pairs = [(query_ref.at[at], query_buf.at[at]), (pair_ref.at[at], pair_buf.at[at])]
            pairs += [(x.at[at], side_buf[0].at[at, i]) for i, x in enumerate(side_refs)]
            pairs += [(x.at[at], corner_buf[0].at[at, i]) for i, x in enumerate(corner_refs)]
            return [pltpu.make_async_copy(x, y, own_sem.at[at, i]) for i, (x, y) in enumerate(pairs)]

        def edge_copies(at, slot):
            return [
                pltpu.make_async_copy(x.at[slot], edge_buf.at[at, i], edge_sem.at[at, i])
                for i, x in enumerate(edge_refs)
            ]

        def begin_own(at, carry):
            for copy in own_copies(at):
                copy.start()
            slot = meta_ref[4, first + at]

            if edges:
                for copy in edge_copies(at, jnp.minimum(slot, edges[0].shape[0] - 1)):
                    copy.start()

            return carry

        def given_copy(g):
            return pltpu.make_async_copy(given_refs[g], given_bufs[g], given_sem.at[g])

        def columns(at):
            return pl.ds(pl.multiple_of(at * block, block), block)

        def weight_copy(index, part, source):
            row = pl.multiple_of(meta_ref[6, places[index][0]] * HEAD_DIM, HEAD_DIM)
            wide = pl.ds(pl.multiple_of(part * part_width, part_width), part_width)
            return pltpu.make_async_copy(
                source.at[pl.ds(row, HEAD_DIM), wide],
                weight_buf.at[pl.ds(index * HEAD_DIM, HEAD_DIM), wide],
                weight_sem.at[index, part],
            )

        def total_copy(at):
            return pltpu.make_async_copy(total_ref.at[:, columns(at)], total_buf.at[:, columns(at)], total_sem.at[at])

        def out_copy(at):
            return pltpu.make_async_copy(out_buf.at[:, columns(at)], out_ref.at[:, columns(at)], out_sem.at[at])

        def begin_share(part, carry):
            for index in range(depth):
                mine = meta_ref[5, places[index][0]] == flag_ref[4]

                @pl.when(mine)
                def _():
                    weight_copy(index, part, weight_refs[0]).start()

                @pl.when(jnp.logical_not(mine))
                def _():
                    weight_copy(index, part, weight_refs[1]).start()

            if total_ref is not None:
                for at in range(blocks // parts):
                    total_copy(part * (blocks // parts) + at).start()
            return carry

        def tile_rows(at, size=1):
            return pl.ds(pl.multiple_of(at * tile, tile), size * tile)

        def off(ok):
            return jnp.where(ok, 0.0, NEG_FILL)

        def lay(row, source_k, source_v):
            key_buf[tile_rows(row), :] = source_k
            value_buf[tile_rows(row), :] = source_v

        def head_step(head, carry):
            place = first + head
            rad_f, rad_r, rad_c = meta_ref[1, place], meta_ref[2, place], meta_ref[3, place]
            for copy in own_copies(head) + edge_copies(head, 0):
                copy.wait()
            col_mask = mask_ref[rad_c]
            side_bias = [None] + [off((rad_f > 0) & (flag_ref[i] != 0)) for i in range(across - 1)]
            bodies = [pair_buf.at[head]] + [side_buf[0].at[head, i] for i in range(across - 1)]

            def band_bias(at):
                low = off((rad_r > 0) & ((at > 0) | (flag_ref[2] != 0)))
                high = off((rad_r > 0) & ((at < tiles - 1) | (flag_ref[3] != 0)))
                return low, None, high

            def run(at, start, biases, flip):
                rows, held = tile_rows(at), tile_rows(start, len(biases))
                attended[head, rows, :] = attend(
                    query_buf[head, 0, rows, :], key_buf[held, :], value_buf[held, :], col_mask, biases, flip
                )

            def fill(band):
                def step(at, carry):
                    rows = tile_rows(at)
                    for which, body in enumerate(bodies):
                        lay(across * (at + band) + which, body[0, rows, :], body[1, rows, :])
                    return carry

                lax.fori_loop(0, tiles, step, 0, unroll=2)

            def with_rows():
                ends = [(edge_buf.at[head, 2 * i], edge_buf.at[head, 2 * i + 1]) for i in range(len(edges) // 2)]
                if corners:
                    ends.append((corner_buf[0].at[head, 0], corner_buf[0].at[head, 1]))
                for which, (low, high) in enumerate(ends):
                    lay(which, low[0], low[1])
                    lay(across * (tiles + 1) + which, high[0], high[1])
                fill(1)

                def each(at, carry):
                    biases = []
                    for x in band_bias(at):
                        for y in side_bias:
                            biases.append(x if y is None else y if x is None else jnp.minimum(x, y))
                    run(at, across * at, biases, across > 1)
                    return carry

                lax.fori_loop(0, tiles, each, 0, unroll=tiles if across == 1 else unroll)

            if sides:
                if edges:
                    pl.when(rad_r > 0)(with_rows)

                @pl.when((rad_r == 0) if edges else True)
                def _():
                    fill(0)

                    def each(at, carry):
                        run(at, across * at, side_bias, False)
                        return carry

                    lax.fori_loop(0, tiles, each, 0, unroll=tiles)

            else:
                with_rows()
            return carry

        def share(part, carry):
            for index in range(depth):
                weight_copy(index, part, weight_refs[0]).wait()

            def each(i, carry):
                at = part * (blocks // parts) + i
                held = [attended[i] if g is None else given_bufs[g][i] for _, g, i in places]
                left = jnp.concatenate(held, axis=1)
                total = jnp.dot(left, weight_buf[:, columns(at)], preferred_element_type=jnp.float32)
                if total_ref is not None:
                    total_copy(at).wait()
                    total += total_buf[:, columns(at)]
                out_buf[:, columns(at)] = total.astype(out_buf.dtype)
                out_copy(at).start()
                return carry

            return lax.fori_loop(0, blocks // parts, each, carry)

        def end_share(at, carry):
            out_copy(at).wait()
            return carry

        if own:
            lax.fori_loop(0, count, begin_own, 0)
        for g in range(len(given)):
            given_copy(g).start()
        if weights:
            lax.fori_loop(0, parts, begin_share, 0)
        if own:
            lax.fori_loop(0, count, head_step, 0)
        for g in range(len(given)):
            given_copy(g).wait()
        if weights:
            lax.fori_loop(0, parts, share, 0)
            lax.fori_loop(0, blocks, end_share, 0)
        else:
            done = pltpu.make_async_copy(attended, out_ref, own_sem.at[0, 0])
            done.start()
            done.wait()

    anywhere, smem = pl.BlockSpec(memory_space=pl.ANY), pl.BlockSpec(memory_space=pltpu.SMEM)
    operands, scratch = [], []
    bf16 = jnp.bfloat16
    if own:
        operands += [own["query"], own["pair"], *sides, *corners, *edges]
        kinds = 2 + len(sides) + len(corners)
        scratch += [
            pltpu.VMEM(own["query"].shape, bf16),
            pltpu.VMEM(own["pair"].shape, bf16),
            pltpu.VMEM((count, max(len(edges), 1), 2, tile, HEAD_DIM), bf16),
            pltpu.VMEM((across * (tiles + 2) * tile, HEAD_DIM), bf16),
            pltpu.VMEM((across * (tiles + 2) * tile, HEAD_DIM), bf16),
            pltpu.VMEM((count, tokens, HEAD_DIM), bf16),
            pltpu.SemaphoreType.DMA((count, kinds)),
            pltpu.SemaphoreType.DMA((count, max(len(edges), 1))),
        ]
    if sides:
        scratch.append(pltpu.VMEM((count, 2, 2, tokens, HEAD_DIM), bf16))
    if corners:
        scratch.append(pltpu.VMEM((count, 2, 2, tile, HEAD_DIM), bf16))
    operands += [x for _, x in given]
    scratch += [pltpu.VMEM(x.shape, bf16) for _, x in given]
    if given:
        scratch.append(pltpu.SemaphoreType.DMA((len(given),)))
    out_type = bf16 if last or not weights else jnp.float32
    if weights:
        operands += list(weights)
        scratch += [
            pltpu.VMEM((depth * HEAD_DIM, width), bf16),
            pltpu.SemaphoreType.DMA((depth, parts)),
            pltpu.VMEM((tokens, width), out_type),
            pltpu.SemaphoreType.DMA((blocks,)),
        ]
    if total_in is not None:
        operands.append(total_in)
        scratch += [pltpu.VMEM((tokens, width), jnp.float32), pltpu.SemaphoreType.DMA((blocks,))]
    shape = (tokens, width) if weights else (count, tokens, HEAD_DIM)
    return pl.pallas_call(
        kernel,
        out_shape=jax.ShapeDtypeStruct(shape, out_type),
        in_specs=[smem, smem, pl.BlockSpec(memory_space=pltpu.VMEM)] + [anywhere] * len(operands),
        out_specs=anywhere,
        scratch_shapes=scratch,
        compiler_params=pltpu.CompilerParams(vmem_limit_bytes=VMEM_BYTES),
    )(meta, flags, col_masks, *operands)


def on_device(queries, keys, values, out_weight, window_radii, frame_valid):
    _, rows_dev, col_total, width = queries.shape
    heads = width // HEAD_DIM
    tile = ROW_TILE * col_total
    tiles = rows_dev // ROW_TILE
    tokens = tile * tiles
    frame_pairs, height_total = lax.axis_size("frame"), lax.axis_size("height")
    q, k, v = (x.reshape(tokens, width) for x in (queries, keys, values))
    outer_pairs = [(2 * i + 1, 2 * i + 2) for i in range(frame_pairs - 1)]
    outer_pairs += [(target, source) for source, target in outer_pairs]
    swap = [(0, 1), (1, 0)]
    down = [(i, i + 1) for i in range(height_total - 1)]
    up = [(i + 1, i) for i in range(height_total - 1)]
    levels = [(heads, heads, heads), (14, 11, 16), (11, 8, 15), (9, 6, 13)]

    meta, slots, flags, level = plan_heads(window_radii.T, frame_valid, levels)
    order = meta[0]

    col = np.arange(tile) % col_total // COL_TILE
    gap = np.abs(col[:, None] - col[None, :])
    col_masks = jnp.asarray(np.stack([np.where(gap <= x, 0.0, NEG_FILL) for x in range(2)]).astype(np.float32))

    def trade_edges(low, high):
        return lax.ppermute(high, "height", down), lax.ppermute(low, "height", up)

    def to_sibling(pair):
        return tuple(lax.ppermute(x, "head", swap) for x in pair)

    def trade_corners(beyond):
        return (
            lax.ppermute(beyond[:, :, tokens - tile :], "height", down),
            lax.ppermute(beyond[:, :, :tile], "height", up),
        )

    def finish(side_count, both_count, edge_count):
        def call(q, k, v, out_weight):
            size = both_count if both_count < side_count else side_count // 2
            parts = [(0, size), (size, side_count - size)]
            rest = heads - side_count
            *packed, low, high = pack_heads(
                order, (k, v), [(*x, (0, 1)) for x in parts], tile, tiles, slots, [(0, edge_count)]
            )
            beyond = [lax.ppermute(x, GRID_AXES, outer_pairs) for x in packed]
            beside = [lax.ppermute(x, "head", swap) for x in packed]
            weights = (out_weight, lax.ppermute(out_weight, "head", swap))
            edges = trade_edges(low, high)
            groups = [(*x, (0,)) for x in parts]
            groups += [(side_count, rest, (0,)), (side_count, rest, (1, 2))] if rest else []
            ordered = pack_heads(order, (q, k, v), groups, tile, tiles)
            edges, ordered = lax.optimization_barrier((edges, ordered))
            edges += to_sibling(edges)
            edges, ordered = lax.optimization_barrier((edges, ordered))
            common = (meta, flags, col_masks)
            shared = []
            near = beyond[0]
            if rest:
                own = {"query": ordered[2], "pair": ordered[3], "edges": edges[:2]}
                lone = chunk(*common, side_count, own, [], (), None, False, tile, tiles)
                near, lone = lax.optimization_barrier((near, lone))
            corners = trade_corners(near)
            total = None
            if rest:
                total = chunk(*common, 0, None, [(side_count, lone)], weights, None, False, tile, tiles)
                corners, total = lax.optimization_barrier((corners, total))
            own = {"query": ordered[0], "pair": packed[0], "sides": (beside[0], near), "edges": edges, "corners": corners}
            first = chunk(*common, 0, own, [], (), None, False, tile, tiles, 4)
            far, first = lax.optimization_barrier((beyond[1], first))
            shared.append((0, first))
            own = {"query": ordered[1], "pair": packed[1], "sides": (beside[1], far), "edges": ()}
            if both_count > size:
                own.update({"edges": edges, "corners": trade_corners(far)})
            return chunk(*common, size, own, shared, weights, total, True, tile, tiles)

        return call

    projected = lax.switch(level[0], [finish(*x) for x in levels], q, k, v, out_weight)
    return projected.reshape(1, rows_dev, col_total, out_weight.shape[1])


def solution(mesh):
    return jax.shard_map(
        on_device,
        mesh=mesh,
        in_specs=(
            P(("frame", "head"), "height", None, None),
            P(("frame", "head"), "height", None, None),
            P(("frame", "head"), "height", None, None),
            P("head", None),
            P(),
            P(),
        ),
        out_specs=P(("frame", "head"), "height", None, None),
        check_vma=False,
    )
```
